32 devices in a mesh: tile: 8 (over y, x, core), comp: 4 (over z).
Axes of the slice: x: 2, y: 2, z: 4, core: 2. Of those that a mesh axis runs over, the one named last changes fastest.
Arguments:
- spectrum: bfloat16 [768, 64, 1024], P('comp', 'tile'), may hold values from 0.049804688 to 2
- sea_mask: int32 [64, 1024], P('tile'), may hold values 0 or 1
- depth_class: int32 [64, 1024], P('tile'), may hold values from 0 to 15
- group_speed: float32 [16, 32], replicated, may hold values from 0.2 to 0.45
- wind_speed: float32 [64, 1024], P('tile'), may hold values from 2 to 20
- wind_dir: float32 [64, 1024], P('tile'), may hold values from -3.140625 to 3.140625
- coupling: bfloat16 [768, 768], replicated, may hold values from -0.21875 to 0.21875
Outputs:
- spectrum_next: bfloat16 [768, 64, 1024], P('comp', 'tile')
The draws below stay inside these ranges and needn't reach their ends.
All inputs are finite; a program needn't handle non-finite values. No bound on the sum of `sea_mask` on one device may be relied on, other than what follows from the above.
Results may differ from the reference program's by a relative error of at most 0.002.
The reference program's roundings to bfloat16 on the way count: a program that leaves them out, or rounds other values in their place, can miss the bound.
Values may be sent and summed in bfloat16 or wider, within the bound.
No kernel may reach another device: no remote copies, remote signals or barrier semaphores. Data moves between devices by JAX's collectives and lax.ppermute only.
A program may use at most 64 MiB of HBM per device.

```python
import math
import jax
import jax.numpy as jnp
from jax import lax

K = 24
F = 32
DEPTHS = 16
PSTEPS = 4
SRC_STEPS = 4
NY = 1024
COMPONENTS = 768
NX = 64


def with_ends(result, key, low, high):
    longest = result.shape.index(max(result.shape))
    spots = []
    for shift in (0, 1):
        where = [jax.random.randint(jax.random.fold_in(key, axis), (), 0, length) for axis, length in enumerate(result.shape)]
        where[longest] = (where[longest] + shift) % result.shape[longest]
        spots.append(tuple(where))
    return result.at[spots[0]].set(low).at[spots[1]].set(high)


def block_levels(own_key, extent, cuts, low, largest):
    def one(dim, blocks):
        draws = jax.random.uniform(jax.random.fold_in(jax.random.fold_in(own_key, 6), dim), (blocks,), jnp.float32, low / len(cuts), largest / len(cuts))
        return jnp.repeat(jnp.exp(draws), extent[dim] // blocks).reshape((-1,) + (1,) * (len(extent) - dim - 1))

    factor_of = one(*cuts[0])
    for cut in cuts[1:]:
        factor_of = factor_of * one(*cut)
    return factor_of


def centred(rng, extent, scale, most, dtype=jnp.bfloat16):
    entries = scale * jax.random.normal(rng, extent, jnp.float32)
    return jnp.clip(entries, min=-most, max=most).astype(dtype)


def setup_inputs(seed: int = 0) -> dict:
    splits = jax.random.split(jax.random.key(seed), 8)
    spectrum = jnp.clip(jnp.exp(math.log(2.0) - 3.6927934 * jax.random.uniform(splits[0], (COMPONENTS, NX, NY), jnp.float32) ** block_levels(splits[0], (COMPONENTS, NX, NY), ((0, 4), (1, 8)), -0.2, 0.2)), 0.049804688, 2.0).astype(jnp.bfloat16)
    sea_mask = with_ends((jax.random.randint(splits[1], (NX, NY), 0, 10) < 7).astype(jnp.int32), jax.random.fold_in(splits[1], 1), 0, 1)
    depth_class = with_ends(jax.random.randint(splits[2], (NX, NY), 0, DEPTHS), jax.random.fold_in(splits[2], 1), 0, DEPTHS - 1).astype(jnp.int32)
    group_speed = jnp.clip(jnp.exp(jax.random.uniform(splits[3], (DEPTHS, F), jnp.float32, math.log(0.2), math.log(0.45))), 0.2, 0.45)
    wind_speed = jnp.clip(jnp.exp(math.log(20.0) - 2.3025851 * jax.random.uniform(splits[4], (NX, NY), jnp.float32) ** block_levels(splits[4], (NX, NY), ((0, 8),), -0.2, 0.2)), 2.0, 20.0)
    wind_dir = jnp.clip(jax.random.uniform(splits[5], (NX, NY), jnp.float32, -3.140625, 3.140625), -3.140625, 3.140625)
    coupling = centred(splits[6], (COMPONENTS, COMPONENTS), COMPONENTS ** -0.5, 0.21875)
    return dict(spectrum=spectrum, sea_mask=sea_mask, depth_class=depth_class, group_speed=group_speed, wind_speed=wind_speed, wind_dir=wind_dir, coupling=coupling)


def advect(energy, courant_x, courant_y, sea):
    west_side = jnp.roll(energy, 1, axis=1)
    east_side = jnp.roll(energy, -1, axis=1)
    padded = jnp.pad(energy, ((0, 0), (0, 0), (1, 1)))
    south_side = padded[:, :, :-2]
    north_side = padded[:, :, 2:]
    moved = (energy - jnp.maximum(courant_x, 0.0) * (energy - west_side)
             - jnp.minimum(courant_x, 0.0) * (east_side - energy)
             - jnp.maximum(courant_y, 0.0) * (energy - south_side)
             - jnp.minimum(courant_y, 0.0) * (north_side - energy))
    return moved * sea


def sources(spectra, speed, direction, coupling, freq_index, theta):
    state = spectra.astype(jnp.float32)
    weight = (0.1 * jnp.power(1.1, freq_index))[:, None]
    align = jnp.maximum(jnp.cos(theta[:, None] - direction[None, :]), 0.0)
    grow = (0.004 * jnp.power(1.1, freq_index - 16.0))[:, None] * speed[None, :] * align
    freq_rate = ((freq_index + 1.0) / F)[:, None]
    for step in range(SRC_STEPS):
        total = jnp.sum(weight * state, axis=0)
        sat = total / (total + 100.0)
        nonlin = jnp.dot(coupling, state.astype(jnp.bfloat16), preferred_element_type=jnp.float32)
        state = jnp.maximum(state + 0.5 * ((grow - 0.3 * sat[None, :] * freq_rate) * state + 0.25 * nonlin), 0.0)
    return state.astype(jnp.bfloat16)


def reference(spectrum, sea_mask, depth_class, group_speed, wind_speed, wind_dir, coupling):
    sea = sea_mask.astype(jnp.float32)[None]
    theta_dir = jnp.arange(K).astype(jnp.float32) * (2.0 * math.pi / K)
    by_freq = spectrum.reshape(F, K, NX, NY)

    def propagate(args):
        block, freq = args
        speed = group_speed[depth_class, freq]
        courant_x = speed[None] * jnp.cos(theta_dir)[:, None, None]
        courant_y = speed[None] * jnp.sin(theta_dir)[:, None, None]
        energy = block.astype(jnp.float32)
        for step in range(PSTEPS):
            energy = advect(energy, courant_x, courant_y, sea)
        return energy.astype(jnp.bfloat16)

    propagated = lax.map(propagate, (by_freq, jnp.arange(F).astype(jnp.int32)))
    propagated = propagated.reshape(COMPONENTS, NX, NY)
    comp_index = jnp.arange(COMPONENTS).astype(jnp.int32)
    freq_index = (comp_index // K).astype(jnp.float32)
    theta = (comp_index % K).astype(jnp.float32) * (2.0 * math.pi / K)
    rows_first = jnp.moveaxis(propagated, 1, 0)

    def update(args):
        column, speed, direction = args
        return sources(column, speed, direction, coupling, freq_index, theta)

    updated = lax.map(update, (rows_first, wind_speed, wind_dir))
    return jnp.moveaxis(updated, 0, 1)
```

```python
import functools
import math

import jax
import jax.numpy as jnp
import numpy as np
from jax import lax
from jax.experimental import pallas as pl
from jax.experimental.pallas import tpu as pltpu
from jax.sharding import PartitionSpec as P

K = 24
F = 32
PSTEPS = 4
SRC_STEPS = 4
PAIR = 2 * K
LANES = 128
VMEM_LIMIT = 48 * 1024 * 1024

THETA = np.arange(K).astype(np.float32) * np.float32(2.0 * math.pi / K)
COS = np.cos(THETA)
SIN = np.sin(THETA)


def eastward_rows(start, count):
    k = lax.rem(start + lax.broadcasted_iota(jnp.int32, (count, 1), 0), K)
    return (k < 6) | (k >= 18)


def pack_kernel(raw, to_east, to_west):
    for out, runs, low in ((to_east, ((0, 6), (18, 24)), 4), (to_west, ((6, 18),), 0)):
        at = 0
        for first, last in runs:
            one = raw[first:last].astype(jnp.float32)
            two = raw[K + first : K + last].astype(jnp.float32)
            row = lax.broadcasted_iota(jnp.int32, one.shape, 1)
            if low:
                both = jnp.where(row < 4, pltpu.roll(one, 4, 1), two)
            else:
                both = jnp.where(row < 4, one, pltpu.roll(two, 4, 1))
            out[at : at + last - first] = both.astype(jnp.bfloat16)
            at += last - first


def pack_halo(spectrum):
    comps, columns, rows = spectrum.shape
    half = jax.ShapeDtypeStruct((comps // 4, columns, rows), jnp.bfloat16)
    block = pl.BlockSpec((K // 2, columns, rows), lambda i: (i, 0, 0))
    return pl.pallas_call(
        pack_kernel,
        grid=(comps // PAIR,),
        in_specs=[pl.BlockSpec((PAIR, columns, rows), lambda i: (i, 0, 0))],
        out_specs=[block, block],
        out_shape=[half, half],
        compiler_params=pltpu.CompilerParams(vmem_limit_bytes=VMEM_LIMIT),
        name="pack_halo",
    )(spectrum)


def propagate_kernel(with_halo, parts, pos, *refs):
    if with_halo:
        raw, west, east, code, code_west, code_east, table, trig = refs[:8]
        refs = refs[8:]
    else:
        raw, code, table, trig = refs[:4]
        refs = refs[4:]
    outs, (cols, speed, result) = refs[: len(parts)], refs[len(parts) :]
    columns, rows = code.shape
    tiles = rows // LANES
    nfreq = table.shape[0]
    step = pl.program_id(0)
    row8 = lax.broadcasted_iota(jnp.int32, (columns, rows), 0)

    for f in range(2):
        for first, last, eastward in ((0, 6, True), (6, 18, False), (18, 24, True)):
            a, b = f * K + first, f * K + last
            own = raw[a:b].astype(jnp.float32)
            if with_halo:
                at = {0: 0, 6: 0, 18: 6}[first]
                side = (west if eastward else east)[at : at + last - first].astype(jnp.float32)
                row = lax.broadcasted_iota(jnp.int32, own.shape, 1)
                own = pltpu.roll(own, 4, 1)
                if eastward:
                    side = pltpu.roll(side, 4, 1) if f else side
                    own = jnp.where(row < 4, side, own)
                else:
                    side = side if f else pltpu.roll(side, 4, 1)
                    own = jnp.where(row < 4, own, side)
            own = own.reshape(-1, rows)
            for t in range(tiles):
                cols[t, a * 8 : b * 8, :] = own[:, t * LANES : (t + 1) * LANES]

    if with_halo:
        turned = pltpu.roll(code[...], 4, 0)
        codes = (
            jnp.where(row8 < 4, pltpu.roll(code_west[...], 4, 0), turned),
            jnp.where(row8 < 4, turned, pltpu.roll(code_east[...], 4, 0)),
        )
    else:
        codes = (code[...],)
    lane = lax.broadcasted_iota(jnp.int32, (8, rows), 1)
    freq0 = step * 2
    for f in range(2):
        line = jnp.broadcast_to(table[freq0 + f], (8, LANES))
        for n, c in enumerate(codes):
            sea = (c >= 16).astype(jnp.float32)
            depth = jnp.bitwise_and(c, 15)
            looked = [
                jnp.take_along_axis(line, depth[:, t * LANES : (t + 1) * LANES], axis=1)
                for t in range(tiles)
            ]
            speed[2 * n] = jnp.concatenate(looked, axis=1) * sea
            speed[2 * n + 1] = sea
        last_n = len(codes) - 1
        for g in range(3):
            base = (f * K + g * 8) * 8

            def column(p):
                return jnp.concatenate(
                    [cols[t, pl.ds(base + p, 8, stride=8), :] for t in range(tiles)], axis=1
                )

            east_rows = eastward_rows(g * 8, 8)

            def upwind_order(get, p):
                if g == 1:
                    return get(1, 7 - p)
                return jnp.where(east_rows, get(0, p), get(1, 7 - p))

            def spread(which):
                def get(side, p):
                    n = side if last_n else 0
                    return jnp.broadcast_to(speed[2 * n + which, p : p + 1, :], (8, rows))

                return get

            k = g * 8 + lax.broadcasted_iota(jnp.int32, (8, rows), 0)
            south = k < 12
            cos = jnp.concatenate([trig[0, g * 8 : g * 8 + 8, :]] * tiles, axis=1)
            sin = jnp.concatenate([trig[1, g * 8 : g * 8 + 8, :]] * tiles, axis=1)
            edge = (south & (lane == 0)) | (~south & (lane == rows - 1))
            inner_sin = jnp.where(edge, 0.0, sin)

            def behind(e):
                if g == 0:
                    return pltpu.roll(e, 1, 1)
                if g == 2:
                    return pltpu.roll(e, rows - 1, 1)
                return jnp.where(south, pltpu.roll(e, 1, 1), pltpu.roll(e, rows - 1, 1))

            before = None
            for p in range(8):
                now = [upwind_order(lambda side, q: column(q), p)]
                if p:
                    rate = upwind_order(spread(0), p)
                    sea = upwind_order(spread(1), p)
                    keep = sea - rate * (cos + sin)
                    from_x = rate * cos
                    from_y = rate * inner_sin
                    for t in range(1, min(p, PSTEPS) + 1):
                        e = now[t - 1]
                        now.append(keep * e + from_x * before[t - 1] + from_y * behind(e))
                if p >= PSTEPS:
                    result[p - PSTEPS, f * K + g * 8 : f * K + g * 8 + 8, :] = now[PSTEPS]
                before = now

    z = pos[0]
    width = rows // pos_count(parts)
    for out, (s, lo, size) in zip(outs, parts):
        at = pl.multiple_of(jnp.bitwise_xor(z, s) * width + lo, LANES)
        out[...] = result[:, :, pl.ds(at, size)].astype(jnp.bfloat16)


def pos_count(parts):
    return max(s for s, _, _ in parts) + 1


def propagate(z, spectrum, code, table, trig, parts, halo=None):
    comps, columns, rows = spectrum.shape
    whole = lambda a: pl.BlockSpec(a.shape, lambda i, z: (0,) * a.ndim)
    blocked = lambda a, n: pl.BlockSpec((n,) + a.shape[1:], lambda i, z: (i, 0, 0))
    args, specs = [spectrum], [blocked(spectrum, PAIR)]
    if halo is not None:
        west, east, code_west, code_east = halo
        args += [west, east, code, code_west, code_east]
        specs += [blocked(west, K // 2), blocked(east, K // 2), whole(code), whole(code), whole(code)]
    else:
        args += [code]
        specs += [whole(code)]
    args += [table, trig]
    specs += [whole(table), whole(trig)]
    return pl.pallas_call(
        functools.partial(propagate_kernel, halo is not None, parts),
        grid_spec=pltpu.PrefetchScalarGridSpec(
            num_scalar_prefetch=1,
            grid=(comps // PAIR,),
            in_specs=specs,
            out_specs=[pl.BlockSpec((4, PAIR, size), lambda i, z: (0, i, 0)) for _, _, size in parts],
            scratch_shapes=[
                pltpu.VMEM((rows // LANES, PAIR * columns, LANES), jnp.float32),
                pltpu.VMEM((4, columns, rows), jnp.float32),
                pltpu.VMEM((4, PAIR, rows), jnp.float32),
            ],
        ),
        out_shape=[jax.ShapeDtypeStruct((4, comps, size), jnp.bfloat16) for _, _, size in parts],
        compiler_params=pltpu.CompilerParams(vmem_limit_bytes=VMEM_LIMIT),
        cost_estimate=pl.CostEstimate(flops=comps * columns * rows * 30, bytes_accessed=6 * comps * rows * 8, transcendentals=0),
        name="propagate_downwind" if halo is None else "propagate_upwind",
    )(z, *args)


def sources_kernel(count, lane0, pos, *refs):
    first, second = refs[:count], refs[count : 2 * count]
    wind_c, wind_s, coupling, trig, rates = refs[2 * count : 2 * count + 5]
    outs = refs[2 * count + 5 : 3 * count + 5]
    state, rounded, nonlin, wind = refs[3 * count + 5 :]
    comps = first[0].shape[1]
    width = outs[0].shape[3]
    whole = comps * count
    z = pos[0]
    mask = eastward_rows(0, comps)
    for s in range(count):
        at = pl.multiple_of(jnp.bitwise_xor(z, s) * comps, comps)
        down = first[s][0, :, lane0 : lane0 + width].astype(jnp.float32)
        up = second[s][0].astype(jnp.float32)
        state[pl.ds(at, comps), 0:width] = jnp.where(mask, up, down)
        state[pl.ds(at, comps), width : 2 * width] = jnp.where(mask, down, up)
    pair = pl.program_id(0)
    for n, x in enumerate((pair, 7 - pair)):
        c = wind_c[x, :, lane0 : lane0 + width]
        d = wind_s[x, :, lane0 : lane0 + width]
        wind[:, n * width : (n + 1) * width] = jnp.maximum(trig[0, :, 0:1] * c + trig[1, :, 0:1] * d, 0.0)

    for step in range(SRC_STEPS):
        total = jnp.zeros((8, 2 * width), jnp.float32)
        for f in range(F):
            here = state[f * K : (f + 1) * K, :]
            rounded[f * K : (f + 1) * K, :] = here.astype(jnp.bfloat16)
            total += float(0.1 * 1.1**f) * (here[0:8] + here[8:16] + here[16:24])
        total = jnp.sum(total, axis=0, keepdims=True)
        sat = total / (total + 100.0)
        nonlin[...] = jnp.dot(coupling[...], rounded[...], preferred_element_type=jnp.float32)
        for f in range(F):
            at = slice(f * K, (f + 1) * K)
            here = state[at, :]
            damp = 1.0 - sat * float(0.15 * (f + 1) / F)
            gain = damp + wind[...] * float(1.1 ** (f - 16))
            state[at, :] = jnp.maximum(gain * here + 0.125 * nonlin[at, :], 0.0)

    for s in range(count):
        at = pl.multiple_of(jnp.bitwise_xor(z, s) * comps, comps)
        for n in range(2):
            outs[s][n, 0] = state[pl.ds(at, comps), n * width : (n + 1) * width].astype(jnp.bfloat16)


def sources(z, first, second, wind_c, wind_s, coupling, trig, lane0):
    count = len(first)
    comps, width = second[0].shape[1], second[0].shape[2]
    whole = lambda a: pl.BlockSpec(a.shape, lambda i, z: (0,) * a.ndim)
    return pl.pallas_call(
        functools.partial(sources_kernel, count, lane0),
        grid_spec=pltpu.PrefetchScalarGridSpec(
            num_scalar_prefetch=1,
            grid=(4,),
            in_specs=[pl.BlockSpec((1,) + a.shape[1:], lambda i, z: (3 - i, 0, 0)) for a in first]
            + [pl.BlockSpec((1,) + a.shape[1:], lambda i, z: (i, 0, 0)) for a in second]
            + [whole(wind_c), whole(wind_s), whole(coupling), whole(trig), whole(trig)],
            out_specs=[pl.BlockSpec((2, 1, comps, width), lambda i, z: (0, i, 0, 0))] * count,
            scratch_shapes=[
                pltpu.VMEM((comps * count, 2 * width), jnp.float32),
                pltpu.VMEM((comps * count, 2 * width), jnp.bfloat16),
                pltpu.VMEM((comps * count, 2 * width), jnp.float32),
                pltpu.VMEM((K, 2 * width), jnp.float32),
            ],
        ),
        out_shape=[jax.ShapeDtypeStruct((2, 4, comps, width), jnp.bfloat16)] * count,
        compiler_params=pltpu.CompilerParams(vmem_limit_bytes=VMEM_LIMIT),
        cost_estimate=pl.CostEstimate(
            flops=SRC_STEPS * 2 * (comps * count) ** 2 * 8 * width, bytes_accessed=4 * comps * count * 8 * width, transcendentals=0
        ),
        name="source_terms",
    )(z, *first, *second, wind_c, wind_s, coupling, trig, trig)


def assemble_kernel(count, pos, *refs):
    blocks, out, turned = refs[:count], refs[-2], refs[-1]
    for s in range(count):

        @pl.when(pl.program_id(0) == s)
        def _():
            comps = blocks[s].shape[2]
            for n in range(2):
                for i in range(4):
                    x = i if n == 0 else 7 - i
                    turned[pl.ds(x, comps, stride=8), :] = blocks[s][n, i].astype(jnp.float32)
            out[...] = turned[...].reshape(out.shape).astype(jnp.bfloat16)


def assemble(z, blocks, rows, chunk, chunks, into):
    count = len(blocks)
    comps, width = blocks[0].shape[2], blocks[0].shape[3]
    extra = [] if into is None else [into]
    return pl.pallas_call(
        functools.partial(assemble_kernel, count),
        grid_spec=pltpu.PrefetchScalarGridSpec(
            num_scalar_prefetch=1,
            grid=(count,),
            in_specs=[pl.BlockSpec(b.shape, lambda i, z: (0, 0, 0, 0)) for b in blocks]
            + [pl.BlockSpec(memory_space=pl.ANY)] * len(extra),
            out_specs=pl.BlockSpec((comps, 8, width), lambda i, z: (0, 0, jnp.bitwise_xor(z[0], i) * chunks + chunk)),
            scratch_shapes=[pltpu.VMEM((comps * 8, width), jnp.float32)],
        ),
        out_shape=jax.ShapeDtypeStruct((comps, 8, rows), jnp.bfloat16),
        input_output_aliases={count + 1: 0} if extra else {},
        compiler_params=pltpu.CompilerParams(vmem_limit_bytes=VMEM_LIMIT),
        name="assemble",
    )(z, *blocks, *extra)


def exchange(blocks, axis):
    count = len(blocks)
    return [blocks[0]] + [
        lax.ppermute(blocks[s], axis, [(i, i ^ s) for i in range(count)]) for s in range(1, count)
    ]


def on_device(spectrum, sea_mask, depth_class, group_speed, wind_speed, wind_dir, coupling):
    comps, columns, rows = spectrum.shape
    count = lax.axis_size("comp")
    tiles = lax.axis_size("tile")
    place = lax.axis_index("comp")
    z = place.astype(jnp.int32).reshape(1)
    width = rows // count
    chunks = max(1, width // LANES)
    east = [(i, (i + 1) % tiles) for i in range(tiles)]
    west = [(j, i) for i, j in east]

    code = depth_class + 16 * sea_mask
    freqs = comps // K
    table = lax.dynamic_slice_in_dim(group_speed, place * freqs, freqs, 1).T
    table = jnp.pad(table, ((0, 0), (0, LANES - table.shape[1])))[:, None]
    trig = jnp.broadcast_to(jnp.asarray(np.stack([np.abs(COS), np.abs(SIN)]))[:, :, None], (2, K, LANES))
    signed = jnp.broadcast_to(jnp.asarray(np.stack([COS, SIN]))[:, :, None], (2, K, LANES))
    start = place * width
    speed_part = 0.002 * lax.dynamic_slice_in_dim(wind_speed, start, width, 1)
    dir_part = lax.dynamic_slice_in_dim(wind_dir, start, width, 1)
    wind_c, wind_s = (speed_part * jnp.cos(dir_part))[:, None], (speed_part * jnp.sin(dir_part))[:, None]

    to_east, to_west = pack_halo(spectrum)
    halo = (
        lax.ppermute(to_east, "tile", east),
        lax.ppermute(to_west, "tile", west),
        lax.ppermute(code, "tile", east),
        lax.ppermute(code, "tile", west),
    )
    first = propagate(z, spectrum, code, table, trig, [(s, 0, width) for s in range(count)])
    first = exchange(first, "comp")
    size = width // chunks
    parts = [(s, c * size, size) for c in range(chunks) for s in range(count)]
    second = propagate(z, spectrum, code, table, trig, parts, halo)
    out = None
    for c in range(chunks):
        arrived = exchange(second[c * count : (c + 1) * count], "comp")
        updated = sources(z, first, arrived, wind_c, wind_s, coupling, signed, c * size)
        out = assemble(z, exchange(updated, "comp"), rows, c, chunks, out)
    return out


def solution(mesh):
    placed = (
        P("comp", "tile", None),
        P("tile", None),
        P("tile", None),
        P(),
        P("tile", None),
        P("tile", None),
        P(),
    )
    return jax.shard_map(
        on_device, mesh=mesh, in_specs=placed, out_specs=P("comp", "tile", None), check_vma=False
    )
```

```python
import functools
import math

import jax
import jax.numpy as jnp
import numpy as np
from jax import lax
from jax.experimental import pallas as pl
from jax.experimental.pallas import tpu as pltpu
from jax.sharding import PartitionSpec as P

K = 24
F = 32
PSTEPS = 4
SRC_STEPS = 4
PAIR = 2 * K
LANES = 128
VMEM_LIMIT = 48 * 1024 * 1024

THETA = np.arange(K).astype(np.float32) * np.float32(2.0 * math.pi / K)
COS = np.cos(THETA)
SIN = np.sin(THETA)


def eastward_rows(start, count):
    k = lax.rem(start + lax.broadcasted_iota(jnp.int32, (count, 1), 0), K)
    return (k < 6) | (k >= 18)


def pack_kernel(raw, code, to_east, to_west):
    step = pl.program_id(0)
    for out, runs, low in ((to_east, ((0, 6), (18, 24)), 4), (to_west, ((6, 18),), 0)):
        at = step * (K // 2)
        for first, last in runs:
            one = raw[first:last].astype(jnp.float32)
            two = raw[K + first : K + last].astype(jnp.float32)
            row = lax.broadcasted_iota(jnp.int32, one.shape, 1)
            if low:
                both = jnp.where(row < 4, pltpu.roll(one, 4, 1), two)
            else:
                both = jnp.where(row < 4, one, pltpu.roll(two, 4, 1))
            out[pl.ds(at, last - first)] = both.astype(jnp.bfloat16)
            at += last - first
        out[out.shape[0] - 1] = code[...].astype(jnp.float32).astype(jnp.bfloat16)


def pack_halo(spectrum, code):
    comps, columns, rows = spectrum.shape
    half = jax.ShapeDtypeStruct((comps // 4 + 1, columns, rows), jnp.bfloat16)
    block = pl.BlockSpec(half.shape, lambda i: (0, 0, 0))
    return pl.pallas_call(
        pack_kernel,
        grid=(comps // PAIR,),
        in_specs=[
            pl.BlockSpec((PAIR, columns, rows), lambda i: (i, 0, 0)),
            pl.BlockSpec(code.shape, lambda i: (0, 0)),
        ],
        out_specs=[block, block],
        out_shape=[half, half],
        compiler_params=pltpu.CompilerParams(vmem_limit_bytes=VMEM_LIMIT),
        name="pack_halo",
    )(spectrum, code)


def propagate_kernel(with_halo, parts, skip, pos, *refs):
    if with_halo:
        raw, west, east, code, code_west, code_east, table, trig = refs[:8]
        refs = refs[8:]
    else:
        raw, code, table, trig = refs[:4]
        refs = refs[4:]
    outs, (cols, speed, result) = refs[: len(parts)], refs[len(parts) :]
    columns, rows = code.shape
    tiles = rows // LANES
    nfreq = table.shape[0]
    step = pl.program_id(0)
    row8 = lax.broadcasted_iota(jnp.int32, (columns, rows), 0)

    for f in range(2):
        for first, last, eastward in ((0, 6, True), (6, 18, False), (18, 24, True)):
            a, b = f * K + first, f * K + last
            own = raw[a:b].astype(jnp.float32)
            if with_halo:
                at = {0: 0, 6: 0, 18: 6}[first]
                side = (west if eastward else east)[at : at + last - first].astype(jnp.float32)
                row = lax.broadcasted_iota(jnp.int32, own.shape, 1)
                own = pltpu.roll(own, 4, 1)
                if eastward:
                    side = pltpu.roll(side, 4, 1) if f else side
                    own = jnp.where(row < 4, side, own)
                else:
                    side = side if f else pltpu.roll(side, 4, 1)
                    own = jnp.where(row < 4, own, side)
            own = own.reshape(-1, rows)
            for t in range(tiles):
                cols[t, a * 8 : b * 8, :] = own[:, t * LANES : (t + 1) * LANES]

    if with_halo:
        turned = pltpu.roll(code[...], 4, 0)
        codes = (
            jnp.where(row8 < 4, pltpu.roll(code_west[0].astype(jnp.float32).astype(jnp.int32), 4, 0), turned),
            jnp.where(row8 < 4, turned, pltpu.roll(code_east[0].astype(jnp.float32).astype(jnp.int32), 4, 0)),
        )
    else:
        codes = (code[...],)
    lane = lax.broadcasted_iota(jnp.int32, (8, rows), 1)
    freq0 = (skip + step) * 2
    for f in range(2):
        line = jnp.broadcast_to(table[freq0 + f], (8, LANES))
        for n, c in enumerate(codes):
            sea = (c >= 16).astype(jnp.float32)
            depth = jnp.bitwise_and(c, 15)
            looked = [
                jnp.take_along_axis(line, depth[:, t * LANES : (t + 1) * LANES], axis=1)
                for t in range(tiles)
            ]
            speed[2 * n] = jnp.concatenate(looked, axis=1) * sea
            speed[2 * n + 1] = sea
        last_n = len(codes) - 1
        for g in range(3):
            base = (f * K + g * 8) * 8

            def column(p):
                return jnp.concatenate(
                    [cols[t, pl.ds(base + p, 8, stride=8), :] for t in range(tiles)], axis=1
                )

            east_rows = eastward_rows(g * 8, 8)

            def upwind_order(get, p):
                if g == 1:
                    return get(1, 7 - p)
                return jnp.where(east_rows, get(0, p), get(1, 7 - p))

            def spread(which):
                def get(side, p):
                    n = side if last_n else 0
                    return jnp.broadcast_to(speed[2 * n + which, p : p + 1, :], (8, rows))

                return get

            k = g * 8 + lax.broadcasted_iota(jnp.int32, (8, rows), 0)
            south = k < 12
            cos = jnp.concatenate([trig[0, g * 8 : g * 8 + 8, :]] * tiles, axis=1)
            sin = jnp.concatenate([trig[1, g * 8 : g * 8 + 8, :]] * tiles, axis=1)
            edge = (south & (lane == 0)) | (~south & (lane == rows - 1))
            inner_sin = jnp.where(edge, 0.0, sin)

            def behind(e):
                if g == 0:
                    return pltpu.roll(e, 1, 1)
                if g == 2:
                    return pltpu.roll(e, rows - 1, 1)
                return jnp.where(south, pltpu.roll(e, 1, 1), pltpu.roll(e, rows - 1, 1))

            now = [upwind_order(lambda side, q: column(q), p) for p in range(8)]
            rates = [upwind_order(spread(0), p) for p in range(1, 8)]
            seas = [upwind_order(spread(1), p) for p in range(1, 8)]
            keep = [None] + [sea - rate * (cos + sin) for sea, rate in zip(seas, rates)]
            from_x = [None] + [rate * cos for rate in rates]
            from_y = [None] + [rate * inner_sin for rate in rates]
            for t in range(1, PSTEPS + 1):
                now = [None] * t + [
                    keep[p] * now[p] + from_x[p] * now[p - 1] + from_y[p] * behind(now[p]) for p in range(t, 8)
                ]
            for p in range(PSTEPS, 8):
                result[p - PSTEPS, f * K + g * 8 : f * K + g * 8 + 8, :] = now[p]

    z = pos[0]
    width = rows // pos_count(parts)
    for out, (s, lo, size) in zip(outs, parts):
        at = pl.multiple_of(jnp.bitwise_xor(z, s) * width + lo, LANES)
        out[...] = result[:, :, pl.ds(at, size)].astype(jnp.bfloat16)


def pos_count(parts):
    return max(s for s, _, _ in parts) + 1


def propagate(z, spectrum, code, table, trig, parts, skip, steps, halo=None):
    columns, rows = spectrum.shape[1:]
    comps = steps * PAIR
    whole = lambda a: pl.BlockSpec(a.shape, lambda i, z: (0,) * a.ndim)
    blocked = lambda a, n: pl.BlockSpec((n,) + a.shape[1:], lambda i, z: (skip + i, 0, 0))
    args, specs = [spectrum], [blocked(spectrum, PAIR)]
    if halo is not None:
        west, east = halo
        last = pl.BlockSpec((1, columns, rows), lambda i, z: (west.shape[0] - 1, 0, 0))
        args += [west, east, code, west, east]
        specs += [blocked(west, K // 2), blocked(east, K // 2), whole(code), last, last]
    else:
        args += [code]
        specs += [whole(code)]
    args += [table, trig]
    specs += [whole(table), whole(trig)]
    return pl.pallas_call(
        functools.partial(propagate_kernel, halo is not None, parts, skip),
        grid_spec=pltpu.PrefetchScalarGridSpec(
            num_scalar_prefetch=1,
            grid=(steps,),
            in_specs=specs,
            out_specs=[pl.BlockSpec((4, PAIR, size), lambda i, z: (0, i, 0)) for _, _, size in parts],
            scratch_shapes=[
                pltpu.VMEM((rows // LANES, PAIR * columns, LANES), jnp.float32),
                pltpu.VMEM((4, columns, rows), jnp.float32),
                pltpu.VMEM((4, PAIR, rows), jnp.float32),
            ],
        ),
        out_shape=[jax.ShapeDtypeStruct((4, comps, size), jnp.bfloat16) for _, _, size in parts],
        compiler_params=pltpu.CompilerParams(vmem_limit_bytes=VMEM_LIMIT),
        cost_estimate=pl.CostEstimate(flops=comps * columns * rows * 30, bytes_accessed=6 * comps * rows * 8, transcendentals=0),
        name="propagate_downwind" if halo is None else "propagate_upwind",
    )(z, *args)


def sources_kernel(count, lane0, pos, *refs):
    pieces = len(refs) - 2 * count - 8
    first, refs = refs[:pieces], refs[pieces:]
    second, (wind_c, wind_s, coupling, trig) = refs[:count], refs[count : count + 4]
    outs, (state, rounded, nonlin, wind) = refs[count + 4 : 2 * count + 4], refs[2 * count + 4 :]
    comps, width = second[0].shape[1:]
    whole = comps * count
    z = pos[0]
    mask = eastward_rows(0, comps)
    for s in range(count):
        at = pl.multiple_of(jnp.bitwise_xor(z, s) * comps, comps)
        down = jnp.concatenate([first[n][0, :, lane0 : lane0 + width] for n in range(s, pieces, count)], axis=0)
        down = down.astype(jnp.float32)
        up = second[s][0].astype(jnp.float32)
        state[pl.ds(at, comps), 0:width] = jnp.where(mask, up, down)
        state[pl.ds(at, comps), width : 2 * width] = jnp.where(mask, down, up)
    pair = pl.program_id(0)
    for n, x in enumerate((pair, 7 - pair)):
        c = wind_c[x, :, lane0 : lane0 + width]
        d = wind_s[x, :, lane0 : lane0 + width]
        wind[:, n * width : (n + 1) * width] = jnp.maximum(trig[0, :, 0:1] * c + trig[1, :, 0:1] * d, 0.0)

    for step in range(SRC_STEPS):
        total = jnp.zeros((8, 2 * width), jnp.float32)
        for f in range(F):
            here = state[f * K : (f + 1) * K, :]
            rounded[f * K : (f + 1) * K, :] = here.astype(jnp.bfloat16)
            total += float(0.1 * 1.1**f) * (here[0:8] + here[8:16] + here[16:24])
        total = jnp.sum(total, axis=0, keepdims=True)
        sat = total / (total + 100.0)
        nonlin[...] = jnp.dot(coupling[...], rounded[...], preferred_element_type=jnp.float32)
        for f in range(F):
            at = slice(f * K, (f + 1) * K)
            here = state[at, :]
            damp = 1.0 - sat * float(0.15 * (f + 1) / F)
            gain = damp + wind[...] * float(1.1 ** (f - 16))
            state[at, :] = jnp.maximum(gain * here + 0.125 * nonlin[at, :], 0.0)

    for s in range(count):
        at = pl.multiple_of(jnp.bitwise_xor(z, s) * comps, comps)
        for n in range(2):
            outs[s][n, 0] = state[pl.ds(at, comps), n * width : (n + 1) * width].astype(jnp.bfloat16)


def sources(z, first, second, wind_c, wind_s, coupling, trig, lane0):
    count = len(second)
    comps, width = second[0].shape[1], second[0].shape[2]
    whole = lambda a: pl.BlockSpec(a.shape, lambda i, z: (0,) * a.ndim)
    return pl.pallas_call(
        functools.partial(sources_kernel, count, lane0),
        grid_spec=pltpu.PrefetchScalarGridSpec(
            num_scalar_prefetch=1,
            grid=(4,),
            in_specs=[pl.BlockSpec((1,) + a.shape[1:], lambda i, z: (3 - i, 0, 0)) for a in first]
            + [pl.BlockSpec((1,) + a.shape[1:], lambda i, z: (i, 0, 0)) for a in second]
            + [whole(wind_c), whole(wind_s), whole(coupling), whole(trig)],
            out_specs=[pl.BlockSpec((2, 1, comps, width), lambda i, z: (0, i, 0, 0))] * count,
            scratch_shapes=[
                pltpu.VMEM((comps * count, 2 * width), jnp.float32),
                pltpu.VMEM((comps * count, 2 * width), jnp.bfloat16),
                pltpu.VMEM((comps * count, 2 * width), jnp.float32),
                pltpu.VMEM((K, 2 * width), jnp.float32),
            ],
        ),
        out_shape=[jax.ShapeDtypeStruct((2, 4, comps, width), jnp.bfloat16)] * count,
        compiler_params=pltpu.CompilerParams(vmem_limit_bytes=VMEM_LIMIT),
        cost_estimate=pl.CostEstimate(
            flops=SRC_STEPS * 2 * (comps * count) ** 2 * 8 * width, bytes_accessed=4 * comps * count * 8 * width, transcendentals=0
        ),
        name="source_terms",
    )(z, *first, *second, wind_c, wind_s, coupling, trig)


def assemble_kernel(count, pos, *refs):
    blocks, out, turned = refs[:count], refs[-2], refs[-1]
    for s in range(count):

        @pl.when(pl.program_id(0) == s)
        def _():
            comps = blocks[s].shape[2]
            for n in range(2):
                for i in range(4):
                    x = i if n == 0 else 7 - i
                    turned[pl.ds(x, comps, stride=8), :] = blocks[s][n, i].astype(jnp.float32)
            out[...] = turned[...].reshape(out.shape).astype(jnp.bfloat16)


def assemble(z, blocks, rows, chunk, chunks, into):
    count = len(blocks)
    comps, width = blocks[0].shape[2], blocks[0].shape[3]
    extra = [] if into is None else [into]
    return pl.pallas_call(
        functools.partial(assemble_kernel, count),
        grid_spec=pltpu.PrefetchScalarGridSpec(
            num_scalar_prefetch=1,
            grid=(count,),
            in_specs=[pl.BlockSpec(b.shape, lambda i, z: (0, 0, 0, 0)) for b in blocks]
            + [pl.BlockSpec(memory_space=pl.ANY)] * len(extra),
            out_specs=pl.BlockSpec((comps, 8, width), lambda i, z: (0, 0, jnp.bitwise_xor(z[0], i) * chunks + chunk)),
            scratch_shapes=[pltpu.VMEM((comps * 8, width), jnp.float32)],
        ),
        out_shape=jax.ShapeDtypeStruct((comps, 8, rows), jnp.bfloat16),
        input_output_aliases={count + 1: 0} if extra else {},
        compiler_params=pltpu.CompilerParams(vmem_limit_bytes=VMEM_LIMIT),
        name="assemble",
    )(z, *blocks, *extra)


def exchange(blocks, axis):
    count = len(blocks)
    came = {s: lax.ppermute(blocks[s], axis, [(i, i ^ s) for i in range(count)]) for s in range(count - 1, 0, -1)}
    return [blocks[0]] + [came[s] for s in range(1, count)]


def on_device(spectrum, sea_mask, depth_class, group_speed, wind_speed, wind_dir, coupling):
    comps, columns, rows = spectrum.shape
    count = lax.axis_size("comp")
    tiles = lax.axis_size("tile")
    place = lax.axis_index("comp")
    z = place.astype(jnp.int32).reshape(1)
    width = rows // count
    chunks = max(1, width // LANES)
    east = [(i, (i + 1) % tiles) for i in range(tiles)]
    west = [(j, i) for i, j in east]

    code = depth_class + 16 * sea_mask
    freqs = comps // K
    table = lax.dynamic_slice_in_dim(group_speed, place * freqs, freqs, 1).T
    table = jnp.pad(table, ((0, 0), (0, LANES - table.shape[1])))[:, None]
    trig = jnp.broadcast_to(jnp.asarray(np.stack([np.abs(COS), np.abs(SIN)]))[:, :, None], (2, K, LANES))
    signed = jnp.broadcast_to(jnp.asarray(np.stack([COS, SIN]))[:, :, None], (2, K, LANES))
    start = place * width
    speed_part = 0.002 * lax.dynamic_slice_in_dim(wind_speed, start, width, 1)
    dir_part = lax.dynamic_slice_in_dim(wind_dir, start, width, 1)
    wind_c, wind_s = (speed_part * jnp.cos(dir_part))[:, None], (speed_part * jnp.sin(dir_part))[:, None]

    to_east, to_west = pack_halo(spectrum, code)
    halo = lax.ppermute(to_east, "tile", east), lax.ppermute(to_west, "tile", west)
    pairs = comps // PAIR
    parts = [(s, 0, width) for s in range(count)]
    first = []
    for skip in range(0, pairs, pairs // 2):
        first += exchange(propagate(z, spectrum, code, table, trig, parts, skip, pairs // 2), "comp")
    size = width // chunks
    parts = [(s, c * size, size) for c in range(chunks) for s in range(count)]
    second = propagate(z, spectrum, code, table, trig, parts, 0, pairs, halo)
    out = None
    for c in range(chunks):
        arrived = exchange(second[c * count : (c + 1) * count], "comp")
        updated = sources(z, first, arrived, wind_c, wind_s, coupling, signed, c * size)
        out = assemble(z, exchange(updated, "comp"), rows, c, chunks, out)
    return out


def solution(mesh):
    placed = (
        P("comp", "tile", None),
        P("tile", None),
        P("tile", None),
        P(),
        P("tile", None),
        P("tile", None),
        P(),
    )
    return jax.shard_map(
        on_device, mesh=mesh, in_specs=placed, out_specs=P("comp", "tile", None), check_vma=False
    )
```

```python
import functools
import math

import jax
import jax.numpy as jnp
import numpy as np
from jax import lax
from jax.experimental import pallas as pl
from jax.experimental.pallas import tpu as pltpu
from jax.sharding import PartitionSpec as P

K = 24
F = 32
PSTEPS = 4
SRC_STEPS = 4
PAIR = 2 * K
LANES = 128
VMEM_LIMIT = 48 * 1024 * 1024
SHORT = pl.CostEstimate(flops=1, bytes_accessed=1, transcendentals=0)

THETA = np.arange(K).astype(np.float32) * np.float32(2.0 * math.pi / K)
COS = np.cos(THETA)
SIN = np.sin(THETA)


def eastward_rows(start, count):
    k = lax.rem(start + lax.broadcasted_iota(jnp.int32, (count, 1), 0), K)
    return (k < 6) | (k >= 18)


def pack_kernel(raw, sea, depth, to_east, to_west, code):
    step = pl.program_id(0)
    code[...] = depth[...] + 16 * sea[...]
    for out, runs, low in ((to_east, ((0, 6), (18, 24)), 4), (to_west, ((6, 18),), 0)):
        at = step * (K // 2)
        for first, last in runs:
            one = raw[first:last].astype(jnp.float32)
            two = raw[K + first : K + last].astype(jnp.float32)
            row = lax.broadcasted_iota(jnp.int32, one.shape, 1)
            if low:
                both = jnp.where(row < 4, pltpu.roll(one, 4, 1), two)
            else:
                both = jnp.where(row < 4, one, pltpu.roll(two, 4, 1))
            out[pl.ds(at, last - first)] = both.astype(jnp.bfloat16)
            at += last - first
        out[out.shape[0] - 1] = code[...].astype(jnp.float32).astype(jnp.bfloat16)


def pack_halo(spectrum, sea_mask, depth_class):
    comps, columns, rows = spectrum.shape
    half = jax.ShapeDtypeStruct((comps // 4 + 1, columns, rows), jnp.bfloat16)
    block = pl.BlockSpec(half.shape, lambda i: (0, 0, 0))
    cells = pl.BlockSpec(sea_mask.shape, lambda i: (0, 0))
    return pl.pallas_call(
        pack_kernel,
        grid=(comps // PAIR,),
        in_specs=[
            pl.BlockSpec((PAIR, columns, rows), lambda i: (i, 0, 0)),
            cells,
            cells,
        ],
        out_specs=[block, block, cells],
        out_shape=[half, half, jax.ShapeDtypeStruct(sea_mask.shape, jnp.int32)],
        compiler_params=pltpu.CompilerParams(vmem_limit_bytes=60 * 1024 * 1024),
        name="pack_halo",
    )(spectrum, sea_mask, depth_class)


def propagate_kernel(with_halo, parts, skip, pos, *refs):
    if with_halo:
        raw, west, east, code, code_west, code_east, table, trig = refs[:8]
        refs = refs[8:]
    else:
        raw, code, table, trig = refs[:4]
        refs = refs[4:]
    outs, (cols, speed, result) = refs[: len(parts)], refs[len(parts) :]
    columns, rows = code.shape
    tiles = rows // LANES
    nfreq = table.shape[0]
    step = pl.program_id(0)
    row8 = lax.broadcasted_iota(jnp.int32, (columns, rows), 0)

    for f in range(2):
        for first, last, eastward in ((0, 6, True), (6, 18, False), (18, 24, True)):
            a, b = f * K + first, f * K + last
            own = raw[a:b].astype(jnp.float32)
            if with_halo:
                at = {0: 0, 6: 0, 18: 6}[first]
                side = (west if eastward else east)[at : at + last - first].astype(jnp.float32)
                row = lax.broadcasted_iota(jnp.int32, own.shape, 1)
                own = pltpu.roll(own, 4, 1)
                if eastward:
                    side = pltpu.roll(side, 4, 1) if f else side
                    own = jnp.where(row < 4, side, own)
                else:
                    side = side if f else pltpu.roll(side, 4, 1)
                    own = jnp.where(row < 4, own, side)
            own = own.reshape(-1, rows)
            for t in range(tiles):
                cols[t, a * 8 : b * 8, :] = own[:, t * LANES : (t + 1) * LANES]

    if with_halo:
        turned = pltpu.roll(code[...], 4, 0)
        codes = (
            jnp.where(row8 < 4, pltpu.roll(code_west[0].astype(jnp.float32).astype(jnp.int32), 4, 0), turned),
            jnp.where(row8 < 4, turned, pltpu.roll(code_east[0].astype(jnp.float32).astype(jnp.int32), 4, 0)),
        )
    else:
        codes = (code[...],)
    lane = lax.broadcasted_iota(jnp.int32, (8, rows), 1)
    freq0 = (skip + step) * 2
    for f in range(2):
        line = jnp.broadcast_to(table[freq0 + f], (8, LANES))
        for n, c in enumerate(codes):
            sea = (c >= 16).astype(jnp.float32)
            depth = jnp.bitwise_and(c, 15)
            looked = [
                jnp.take_along_axis(line, depth[:, t * LANES : (t + 1) * LANES], axis=1)
                for t in range(tiles)
            ]
            speed[2 * n] = jnp.concatenate(looked, axis=1) * sea
            speed[2 * n + 1] = sea
        last_n = len(codes) - 1
        for g in range(3):
            base = (f * K + g * 8) * 8

            def column(p):
                return jnp.concatenate(
                    [cols[t, pl.ds(base + p, 8, stride=8), :] for t in range(tiles)], axis=1
                )

            east_rows = eastward_rows(g * 8, 8)

            def upwind_order(get, p):
                if g == 1:
                    return get(1, 7 - p)
                return jnp.where(east_rows, get(0, p), get(1, 7 - p))

            def spread(which):
                def get(side, p):
                    n = side if last_n else 0
                    return jnp.broadcast_to(speed[2 * n + which, p : p + 1, :], (8, rows))

                return get

            k = g * 8 + lax.broadcasted_iota(jnp.int32, (8, rows), 0)
            south = k < 12
            cos = jnp.concatenate([trig[0, g * 8 : g * 8 + 8, :]] * tiles, axis=1)
            sin = jnp.concatenate([trig[1, g * 8 : g * 8 + 8, :]] * tiles, axis=1)
            edge = (south & (lane == 0)) | (~south & (lane == rows - 1))
            inner_sin = jnp.where(edge, 0.0, sin)

            def behind(e):
                if g == 0:
                    return pltpu.roll(e, 1, 1)
                if g == 2:
                    return pltpu.roll(e, rows - 1, 1)
                return jnp.where(south, pltpu.roll(e, 1, 1), pltpu.roll(e, rows - 1, 1))

            now = [upwind_order(lambda side, q: column(q), p) for p in range(8)]
            rates = [upwind_order(spread(0), p) for p in range(1, 8)]
            seas = [upwind_order(spread(1), p) for p in range(1, 8)]
            keep = [None] + [sea - rate * (cos + sin) for sea, rate in zip(seas, rates)]
            from_x = [None] + [rate * cos for rate in rates]
            from_y = [None] + [rate * inner_sin for rate in rates]
            for t in range(1, PSTEPS + 1):
                now = [None] * t + [
                    keep[p] * now[p] + from_x[p] * now[p - 1] + from_y[p] * behind(now[p]) for p in range(t, 8)
                ]
            for p in range(PSTEPS, 8):
                result[p - PSTEPS, f * K + g * 8 : f * K + g * 8 + 8, :] = now[p]

    z = pos[0]
    width = rows // pos_count(parts)
    for out, (s, lo, size) in zip(outs, parts):
        at = pl.multiple_of(jnp.bitwise_xor(z, s) * width + lo, LANES)
        out[...] = result[:, :, pl.ds(at, size)].astype(jnp.bfloat16)


def pos_count(parts):
    return max(s for s, _, _ in parts) + 1


def propagate(z, spectrum, code, table, trig, parts, skip, steps, halo=None):
    columns, rows = spectrum.shape[1:]
    comps = steps * PAIR
    whole = lambda a: pl.BlockSpec(a.shape, lambda i, z: (0,) * a.ndim)
    blocked = lambda a, n: pl.BlockSpec((n,) + a.shape[1:], lambda i, z: (skip + i, 0, 0))
    args, specs = [spectrum], [blocked(spectrum, PAIR)]
    if halo is not None:
        west, east = halo
        last = pl.BlockSpec((1, columns, rows), lambda i, z: (west.shape[0] - 1, 0, 0))
        args += [west, east, code, west, east]
        specs += [blocked(west, K // 2), blocked(east, K // 2), whole(code), last, last]
    else:
        args += [code]
        specs += [whole(code)]
    args += [table, trig]
    specs += [whole(table), whole(trig)]
    return pl.pallas_call(
        functools.partial(propagate_kernel, halo is not None, parts, skip),
        grid_spec=pltpu.PrefetchScalarGridSpec(
            num_scalar_prefetch=1,
            grid=(steps,),
            in_specs=specs,
            out_specs=[pl.BlockSpec((4, PAIR, size), lambda i, z: (0, i, 0)) for _, _, size in parts],
            scratch_shapes=[
                pltpu.VMEM((rows // LANES, PAIR * columns, LANES), jnp.float32),
                pltpu.VMEM((4, columns, rows), jnp.float32),
                pltpu.VMEM((4, PAIR, rows), jnp.float32),
            ],
        ),
        out_shape=[jax.ShapeDtypeStruct((4, comps, size), jnp.bfloat16) for _, _, size in parts],
        compiler_params=pltpu.CompilerParams(vmem_limit_bytes=VMEM_LIMIT),
        cost_estimate=pl.CostEstimate(flops=comps * columns * rows * 30, bytes_accessed=6 * comps * rows * 8, transcendentals=0),
        name="propagate_downwind" if halo is None else "propagate_upwind",
    )(z, *args)


def rank_kernel(sea, ranks, most, mask):
    blocks, span = mask.shape
    width = span // 4
    for r in range(blocks):
        d, g = r // 2, r % 2
        for i in range(4):
            x = 4 + i if g else 3 - i
            mask[r : r + 1, i * width : (i + 1) * width] = sea[x : x + 1, d * width : (d + 1) * width].astype(jnp.float32)
    lane = lax.broadcasted_iota(jnp.int32, mask.shape, 1)
    count = mask[...]
    shift = 1
    while shift < span:
        count += jnp.where(lane >= shift, pltpu.roll(count, shift, 1), 0.0)
        shift *= 2
    place = jnp.where(mask[...] > 0.0, count - 1.0, -1.0).astype(jnp.int32)
    for r in range(blocks):
        ranks[r // 2, r % 2] = place[r : r + 1]
    top = jnp.max(jnp.max(count, axis=1, keepdims=True), axis=0, keepdims=True)
    most[...] = jnp.broadcast_to(top, most.shape).astype(jnp.int32)


def sea_ranks(sea_mask, count):
    span = 4 * (sea_mask.shape[1] // count)
    return pl.pallas_call(
        rank_kernel,
        out_shape=[
            jax.ShapeDtypeStruct((count, 2, 1, span), jnp.int32),
            jax.ShapeDtypeStruct((8, LANES), jnp.int32),
        ],
        scratch_shapes=[pltpu.VMEM((2 * count, span), jnp.float32)],
        cost_estimate=SHORT,
        name="sea_ranks",
    )(sea_mask)


def one_hot(rank, first, size):
    row = first + lax.broadcasted_iota(jnp.int32, (size, rank.shape[1]), 0)
    return jnp.where(row == rank, 1.0, 0.0).astype(jnp.bfloat16)


def pack(values, hot):
    return lax.dot_general(values, hot, (((1,), (1,)), ((), ())), preferred_element_type=jnp.float32)


def pack_points_kernel(downwind, first_block, pos, piece, ranks, *outs):
    comps = piece.shape[1]
    blocks = sum(out.shape[0] for out in outs)
    values = jnp.concatenate([piece[i if downwind else 3 - i] for i in range(4)], axis=1)
    low, high = (
        pack(values, one_hot(ranks[0, g], first_block * LANES, blocks * LANES)) for g in range(2)
    )
    if downwind:
        low, high = high, low
    packed = jnp.where(eastward_rows(0, comps), low, high).astype(jnp.bfloat16)
    at = 0
    for out in outs:
        for j in range(out.shape[0]):
            out[j] = packed[:, at * LANES : (at + 1) * LANES]
            at += 1


def pack_points(z, s, piece, ranks, downwind, first_block, sizes):
    comps = piece.shape[1]
    whole = lambda a: pl.BlockSpec(a.shape, lambda i, z: (0,) * a.ndim)
    outs = [jax.ShapeDtypeStruct((n, comps, LANES), jnp.bfloat16) for n in sizes]
    return pl.pallas_call(
        functools.partial(pack_points_kernel, downwind, first_block),
        grid_spec=pltpu.PrefetchScalarGridSpec(
            num_scalar_prefetch=1,
            grid=(1,),
            in_specs=[
                whole(piece),
                pl.BlockSpec((1,) + ranks.shape[1:], lambda i, z: (jnp.bitwise_xor(z[0], s), 0, 0, 0)),
            ],
            out_specs=[whole(out) for out in outs],
        ),
        out_shape=outs,
        compiler_params=pltpu.CompilerParams(vmem_limit_bytes=VMEM_LIMIT),
        cost_estimate=SHORT,
        name="pack_points",
    )(z, piece, ranks)


def pack_first_kernel(first_block, count, pos, *refs):
    pieces, (ranks, wind_c, wind_s, packed, wind) = refs[:-5], refs[-5:]
    z = pos[0]
    blocks, total, _ = packed.shape
    comps = total // count
    hots = [one_hot(ranks[0, g], first_block * LANES, blocks * LANES) for g in range(2)]
    mask = eastward_rows(0, comps)
    for s in range(count):
        at = pl.multiple_of(jnp.bitwise_xor(z, s) * comps, comps)
        values = jnp.concatenate([pieces[s][i] for i in range(4)], axis=1)
        low, high = (pack(values, hot) for hot in hots)
        both = jnp.where(mask, high, low).astype(jnp.bfloat16)
        for j in range(blocks):
            packed[j, pl.ds(at, comps), :] = both[:, j * LANES : (j + 1) * LANES]
    for g in range(2):
        parts = []
        for source in (wind_c, wind_s):
            left = jnp.concatenate([source[4 + i if g else 3 - i] for i in range(4)], axis=1)
            for _ in range(3):
                part = left.astype(jnp.bfloat16).astype(jnp.float32)
                parts.append(part)
                left = left - part
        parts += [jnp.zeros_like(left)] * 2
        row = pack(jnp.concatenate(parts, axis=0).astype(jnp.bfloat16), hots[g])
        for n in range(2):
            wind[2 * g + n] = row[3 * n : 3 * n + 1] + row[3 * n + 1 : 3 * n + 2] + row[3 * n + 2 : 3 * n + 3]


def pack_first(z, pieces, ranks, wind_c, wind_s, count, first_block, blocks):
    total = sum(piece.shape[1] for piece in pieces)
    whole = lambda a: pl.BlockSpec(a.shape, lambda i, z: (0,) * a.ndim)
    outs = [
        jax.ShapeDtypeStruct((blocks, total, LANES), jnp.bfloat16),
        jax.ShapeDtypeStruct((4, 1, blocks * LANES), jnp.float32),
    ]
    return pl.pallas_call(
        functools.partial(pack_first_kernel, first_block, count),
        grid_spec=pltpu.PrefetchScalarGridSpec(
            num_scalar_prefetch=1,
            grid=(1,),
            in_specs=[whole(piece) for piece in pieces]
            + [pl.BlockSpec((1,) + ranks.shape[1:], lambda i, z: (z[0], 0, 0, 0)), whole(wind_c), whole(wind_s)],
            out_specs=[whole(out) for out in outs],
        ),
        out_shape=outs,
        compiler_params=pltpu.CompilerParams(vmem_limit_bytes=VMEM_LIMIT),
        cost_estimate=SHORT,
        name="pack_first",
    )(z, *pieces, ranks, wind_c, wind_s)


def sources_kernel(count, pos, *refs):
    first, later, refs = refs[0], refs[1 : 1 + count], refs[1 + count :]
    second, (winds, coupling, trig) = refs[:count], refs[count : count + 3]
    outs, (state, rounded, nonlin, wind) = refs[count + 3 : 2 * count + 3], refs[2 * count + 3 :]
    comps, width = second[0].shape[1:]
    z = pos[0]
    mask = eastward_rows(0, comps)
    for s in range(count):
        source = jnp.bitwise_xor(z, s)
        at = pl.ds(pl.multiple_of(source * comps, comps), comps)
        part = comps - later[s].shape[1]
        early = first[0, pl.ds(pl.multiple_of(source * part, part), part), :]
        down = jnp.concatenate([early, later[s][0]], axis=0).astype(jnp.float32)
        up = second[s][0].astype(jnp.float32)
        state[at, 0:width] = jnp.where(mask, up, down)
        state[at, width : 2 * width] = jnp.where(mask, down, up)
    for g in range(2):
        toward = trig[0, :, 0:1] * winds[2 * g] + trig[1, :, 0:1] * winds[2 * g + 1]
        wind[:, g * width : (g + 1) * width] = jnp.maximum(toward, 0.0)

    for step in range(SRC_STEPS):
        total = jnp.zeros((8, 2 * width), jnp.float32)
        for f in range(F):
            here = state[f * K : (f + 1) * K, :]
            rounded[f * K : (f + 1) * K, :] = here.astype(jnp.bfloat16)
            total += float(0.1 * 1.1**f) * (here[0:8] + here[8:16] + here[16:24])
        total = jnp.sum(total, axis=0, keepdims=True)
        sat = total / (total + 100.0)
        nonlin[...] = jnp.dot(coupling[...], rounded[...], preferred_element_type=jnp.float32)
        for f in range(F):
            at = slice(f * K, (f + 1) * K)
            here = state[at, :]
            damp = 1.0 - sat * float(0.15 * (f + 1) / F)
            gain = damp + wind[...] * float(1.1 ** (f - 16))
            state[at, :] = jnp.maximum(gain * here + 0.125 * nonlin[at, :], 0.0)

    for s in range(count):
        at = pl.ds(pl.multiple_of(jnp.bitwise_xor(z, s) * comps, comps), comps)
        for g in range(2):
            outs[s][g, 0] = state[at, g * width : (g + 1) * width].astype(jnp.bfloat16)


def sources(z, first, later, second, winds, coupling, trig, first_block):
    count = len(second)
    blocks, comps, width = second[0].shape
    total = comps * count
    whole = lambda a: pl.BlockSpec(a.shape, lambda i, z: (0,) * a.ndim)
    return pl.pallas_call(
        functools.partial(sources_kernel, count),
        grid_spec=pltpu.PrefetchScalarGridSpec(
            num_scalar_prefetch=1,
            grid=(blocks,),
            in_specs=[pl.BlockSpec((1,) + a.shape[1:], lambda i, z: (first_block + i, 0, 0)) for a in [first, *later]]
            + [pl.BlockSpec((1, comps, width), lambda i, z: (i, 0, 0)) for a in second]
            + [pl.BlockSpec((4, 1, width), lambda i, z: (0, 0, first_block + i)), whole(coupling), whole(trig)],
            out_specs=[pl.BlockSpec((2, 1, comps, width), lambda i, z: (0, i, 0, 0))] * count,
            scratch_shapes=[
                pltpu.VMEM((total, 2 * width), jnp.float32),
                pltpu.VMEM((total, 2 * width), jnp.bfloat16),
                pltpu.VMEM((total, 2 * width), jnp.float32),
                pltpu.VMEM((K, 2 * width), jnp.float32),
            ],
        ),
        out_shape=[jax.ShapeDtypeStruct((2, blocks, comps, width), jnp.bfloat16)] * count,
        compiler_params=pltpu.CompilerParams(vmem_limit_bytes=VMEM_LIMIT),
        cost_estimate=pl.CostEstimate(
            flops=SRC_STEPS * 2 * total**2 * 2 * blocks * width, bytes_accessed=8 * total * blocks * width, transcendentals=0
        ),
        name="source_terms",
    )(z, first, *later, *second, winds, coupling, trig)


def unpack_kernel(partners, first_block, rest_block, scalars, *refs):
    n = len(partners)
    blocks, refs = refs[:n], refs[n:]
    rest = refs[:n] if rest_block else ()
    ranks, (out, turned) = refs[len(rest)], refs[-2:]
    comps, _, width = out.shape
    tiles = width // LANES

    def spread(part, first, add):
        for g in range(2):
            values = jnp.concatenate([part[g, j] for j in range(part.shape[1])], axis=1)
            hot = one_hot(ranks[0, g], first * LANES, values.shape[1])
            wide = jnp.dot(values, hot, preferred_element_type=jnp.float32)
            for i in range(4):
                x = 4 + i if g else 3 - i
                for t in range(tiles):
                    at = i * width + t * LANES
                    here = wide[:, at : at + LANES]
                    if add:
                        here += turned[t, pl.ds(x, comps, stride=8), :]
                    turned[t, pl.ds(x, comps, stride=8), :] = here

    for i in range(n):

        @pl.when(pl.program_id(0) == i)
        def _():
            spread(blocks[i], first_block, False)
            if rest:

                @pl.when(scalars[1] > 0)
                def _():
                    spread(rest[i], rest_block, True)

    for t in range(tiles):
        here = turned[t].reshape(comps, 8, LANES)
        if len(refs) > len(rest) + 3:
            here += refs[len(rest) + 1][:, :, t * LANES : (t + 1) * LANES].astype(jnp.float32)
        out[:, :, t * LANES : (t + 1) * LANES] = here.astype(jnp.bfloat16)


def unpack(scalars, partners, blocks, first_block, rest, rest_block, ranks, rows, into):
    comps = blocks[0].shape[2]
    width = ranks.shape[3] // 4
    whole = lambda a: pl.BlockSpec(a.shape, lambda i, z: (0,) * a.ndim)
    first = partners[0]
    device = lambda i, z: jnp.bitwise_xor(z[0], first + i)
    place = pl.BlockSpec((comps, 8, width), lambda i, z: (0, 0, device(i, z)))
    extra = [] if into is None else [into]
    inputs = [*blocks, *rest]
    return pl.pallas_call(
        functools.partial(unpack_kernel, partners, first_block, rest_block),
        grid_spec=pltpu.PrefetchScalarGridSpec(
            num_scalar_prefetch=1,
            grid=(len(partners),),
            in_specs=[whole(part) for part in inputs]
            + [pl.BlockSpec((1,) + ranks.shape[1:], lambda i, z: (device(i, z), 0, 0, 0))]
            + [place] * len(extra),
            out_specs=place,
            scratch_shapes=[pltpu.VMEM((width // LANES, comps * 8, LANES), jnp.float32)],
        ),
        out_shape=jax.ShapeDtypeStruct((comps, 8, rows), jnp.bfloat16),
        input_output_aliases={len(inputs) + 2: 0} if extra else {},
        compiler_params=pltpu.CompilerParams(vmem_limit_bytes=VMEM_LIMIT),
        cost_estimate=SHORT,
        name="unpack",
    )(scalars, *inputs, ranks, *extra)


def exchange(blocks, axis):
    count = len(blocks)
    came = {s: lax.ppermute(blocks[s], axis, [(i, i ^ s) for i in range(count)]) for s in range(count - 1, 0, -1)}
    return [blocks[0]] + [came[s] for s in range(1, count)]


def exchange_rare(blocks, axis):
    order = jnp.bitwise_xor(lax.axis_index(axis), jnp.arange(len(blocks)))
    came = lax.all_to_all(jnp.stack(blocks)[order], axis, split_axis=0, concat_axis=0, tiled=True)[order]
    return [came[s] for s in range(len(blocks))]


def on_device(spectrum, sea_mask, depth_class, group_speed, wind_speed, wind_dir, coupling):
    comps, columns, rows = spectrum.shape
    count = lax.axis_size("comp")
    tiles = lax.axis_size("tile")
    place = lax.axis_index("comp")
    z = place.astype(jnp.int32).reshape(1)
    width = rows // count
    east = [(i, (i + 1) % tiles) for i in range(tiles)]
    west = [(j, i) for i, j in east]

    freqs = comps // K
    table = lax.dynamic_slice_in_dim(group_speed, place * freqs, freqs, 1).T
    table = jnp.pad(table, ((0, 0), (0, LANES - table.shape[1])))[:, None]
    trig = jnp.broadcast_to(jnp.asarray(np.stack([np.abs(COS), np.abs(SIN)]))[:, :, None], (2, K, LANES))
    signed = jnp.broadcast_to(jnp.asarray(np.stack([COS, SIN]))[:, :, None], (2, K, LANES))
    start = place * width
    speed_part = 0.002 * lax.dynamic_slice_in_dim(wind_speed, start, width, 1)
    dir_part = lax.dynamic_slice_in_dim(wind_dir, start, width, 1)
    wind_c, wind_s = (speed_part * jnp.cos(dir_part))[:, None], (speed_part * jnp.sin(dir_part))[:, None]

    to_east, to_west, code = pack_halo(spectrum, sea_mask, depth_class)
    halo = lax.ppermute(to_east, "tile", east), lax.ppermute(to_west, "tile", west)
    pairs = comps // PAIR
    half = pairs // 2
    blocks = 4 * width // LANES
    main = blocks * 3 // 4
    chunks = 2 if main % 2 == 0 else 1
    size = main // chunks
    parts = [(s, 0, width) for s in range(count)]
    first = exchange(propagate(z, spectrum, code, table, trig, parts, 0, half), "comp")
    later = propagate(z, spectrum, code, table, trig, parts, half, pairs - half)
    ranks, most = sea_ranks(sea_mask, count)
    packed_later = [pack_points(z, s, later[s], ranks, True, 0, [main])[0] for s in range(count)]
    packed_later = exchange(packed_later, "comp")
    second = propagate(z, spectrum, code, table, trig, parts, 0, pairs, halo)
    packed = [pack_points(z, s, second[s], ranks, False, 0, [size] * chunks) for s in range(count)]
    packed_first, winds = pack_first(z, first, ranks, wind_c, wind_s, count, 0, main)

    def remainder(first, later, second, ranks, wind_c, wind_s, coupling):
        rest = blocks - main
        down, winds = pack_first(z, first, ranks, wind_c, wind_s, count, main, rest)
        low = [pack_points(z, s, later[s], ranks, True, main, [rest])[0] for s in range(count)]
        high = [pack_points(z, s, second[s], ranks, False, main, [rest])[0] for s in range(count)]
        low, high = exchange_rare(low, "comp"), exchange_rare(high, "comp")
        return exchange_rare(sources(z, down, low, high, winds, coupling, signed, 0), "comp")

    def nothing(*args):
        return [jnp.zeros((2, blocks - main, comps, LANES), jnp.bfloat16)] * count

    updated = []
    for c in range(chunks):
        arrived = exchange([packed[s][c] for s in range(count)], "comp")
        sent = sources(z, packed_first, packed_later, arrived, winds, coupling, signed, c * size)
        updated.append(exchange(sent, "comp"))
        if c == 0:
            most, _ = lax.optimization_barrier((most, arrived[0]))
            full = lax.pmax(most[0, 0], "tile") > main * LANES
    full, _ = lax.optimization_barrier((full, sent[0]))
    rest = lax.cond(full, remainder, nothing, first, later, second, ranks, wind_c, wind_s, coupling)
    scalars = jnp.concatenate([z, full.astype(jnp.int32).reshape(1)])
    everyone = list(range(count))
    out = unpack(scalars, everyone, updated[0], 0, rest, main, ranks, rows, None)
    for partners in (everyone[: count // 2], everyone[count // 2 :]):
        for c in range(1, chunks):
            out = unpack(scalars, partners, [updated[c][s] for s in partners], c * size, [], 0, ranks, rows, out)
    return out


def solution(mesh):
    placed = (
        P("comp", "tile", None),
        P("tile", None),
        P("tile", None),
        P(),
        P("tile", None),
        P("tile", None),
        P(),
    )
    return jax.shard_map(
        on_device, mesh=mesh, in_specs=placed, out_specs=P("comp", "tile", None), check_vma=False
    )
```

```python
import functools
import math

import jax
import jax.numpy as jnp
import numpy as np
from jax import lax
from jax.experimental import pallas as pl
from jax.experimental.pallas import tpu as pltpu
from jax.sharding import PartitionSpec as P

K = 24
F = 32
PSTEPS = 4
SRC_STEPS = 4
PAIR = 2 * K
LANES = 128
VMEM_LIMIT = 48 * 1024 * 1024
SHORT = pl.CostEstimate(flops=1, bytes_accessed=1, transcendentals=0)

THETA = np.arange(K).astype(np.float32) * np.float32(2.0 * math.pi / K)
COS = np.cos(THETA)
SIN = np.sin(THETA)


def eastward_rows(start, count):
    k = lax.rem(start + lax.broadcasted_iota(jnp.int32, (count, 1), 0), K)
    return (k < 6) | (k >= 18)


def pack_kernel(raw, sea, depth, to_east, to_west, code):
    step = pl.program_id(0)
    code[...] = depth[...] + 16 * sea[...]
    for out, runs, low in ((to_east, ((0, 6), (18, 24)), 4), (to_west, ((6, 18),), 0)):
        at = step * (K // 2)
        for first, last in runs:
            one = raw[first:last].astype(jnp.float32)
            two = raw[K + first : K + last].astype(jnp.float32)
            row = lax.broadcasted_iota(jnp.int32, one.shape, 1)
            if low:
                both = jnp.where(row < 4, pltpu.roll(one, 4, 1), two)
            else:
                both = jnp.where(row < 4, one, pltpu.roll(two, 4, 1))
            out[pl.ds(at, last - first)] = both.astype(jnp.bfloat16)
            at += last - first
        out[out.shape[0] - 1] = code[...].astype(jnp.float32).astype(jnp.bfloat16)


def pack_halo(spectrum, sea_mask, depth_class):
    comps, columns, rows = spectrum.shape
    half = jax.ShapeDtypeStruct((comps // 4 + 1, columns, rows), jnp.bfloat16)
    block = pl.BlockSpec(half.shape, lambda i: (0, 0, 0))
    cells = pl.BlockSpec(sea_mask.shape, lambda i: (0, 0))
    return pl.pallas_call(
        pack_kernel,
        grid=(comps // PAIR,),
        in_specs=[
            pl.BlockSpec((PAIR, columns, rows), lambda i: (i, 0, 0)),
            cells,
            cells,
        ],
        out_specs=[block, block, cells],
        out_shape=[half, half, jax.ShapeDtypeStruct(sea_mask.shape, jnp.int32)],
        compiler_params=pltpu.CompilerParams(vmem_limit_bytes=60 * 1024 * 1024),
        name="pack_halo",
    )(spectrum, sea_mask, depth_class)


def propagate_kernel(with_halo, parts, skip, pos, *refs):
    if with_halo:
        raw, west, east, code, code_west, code_east, table, trig = refs[:8]
        refs = refs[8:]
    else:
        raw, code, table, trig = refs[:4]
        refs = refs[4:]
    outs, (cols, speed, result) = refs[: len(parts)], refs[len(parts) :]
    columns, rows = code.shape
    tiles = rows // LANES
    nfreq = table.shape[0]
    step = pl.program_id(0)
    row8 = lax.broadcasted_iota(jnp.int32, (columns, rows), 0)

    for f in range(2):
        for first, last, eastward in ((0, 6, True), (6, 18, False), (18, 24, True)):
            a, b = f * K + first, f * K + last
            own = raw[a:b].astype(jnp.float32)
            if with_halo:
                at = {0: 0, 6: 0, 18: 6}[first]
                side = (west if eastward else east)[at : at + last - first].astype(jnp.float32)
                row = lax.broadcasted_iota(jnp.int32, own.shape, 1)
                own = pltpu.roll(own, 4, 1)
                if eastward:
                    side = pltpu.roll(side, 4, 1) if f else side
                    own = jnp.where(row < 4, side, own)
                else:
                    side = side if f else pltpu.roll(side, 4, 1)
                    own = jnp.where(row < 4, own, side)
            own = own.reshape(-1, rows)
            for t in range(tiles):
                cols[t, a * 8 : b * 8, :] = own[:, t * LANES : (t + 1) * LANES]

    if with_halo:
        turned = pltpu.roll(code[...], 4, 0)
        codes = (
            jnp.where(row8 < 4, pltpu.roll(code_west[0].astype(jnp.float32).astype(jnp.int32), 4, 0), turned),
            jnp.where(row8 < 4, turned, pltpu.roll(code_east[0].astype(jnp.float32).astype(jnp.int32), 4, 0)),
        )
    else:
        codes = (code[...],)
    lane = lax.broadcasted_iota(jnp.int32, (8, rows), 1)
    freq0 = (skip + step) * 2
    for f in range(2):
        line = jnp.broadcast_to(table[freq0 + f], (8, LANES))
        for n, c in enumerate(codes):
            sea = (c >= 16).astype(jnp.float32)
            depth = jnp.bitwise_and(c, 15)
            looked = [
                jnp.take_along_axis(line, depth[:, t * LANES : (t + 1) * LANES], axis=1)
                for t in range(tiles)
            ]
            speed[2 * n] = jnp.concatenate(looked, axis=1) * sea
            speed[2 * n + 1] = sea
        last_n = len(codes) - 1
        for g in range(3):
            base = (f * K + g * 8) * 8

            def column(p):
                return jnp.concatenate(
                    [cols[t, pl.ds(base + p, 8, stride=8), :] for t in range(tiles)], axis=1
                )

            east_rows = eastward_rows(g * 8, 8)

            def upwind_order(get, p):
                if g == 1:
                    return get(1, 7 - p)
                return jnp.where(east_rows, get(0, p), get(1, 7 - p))

            def spread(which):
                def get(side, p):
                    n = side if last_n else 0
                    return jnp.broadcast_to(speed[2 * n + which, p : p + 1, :], (8, rows))

                return get

            k = g * 8 + lax.broadcasted_iota(jnp.int32, (8, rows), 0)
            south = k < 12
            cos = jnp.concatenate([trig[0, g * 8 : g * 8 + 8, :]] * tiles, axis=1)
            sin = jnp.concatenate([trig[1, g * 8 : g * 8 + 8, :]] * tiles, axis=1)
            edge = (south & (lane == 0)) | (~south & (lane == rows - 1))
            inner_sin = jnp.where(edge, 0.0, sin)

            def behind(e):
                if g == 0:
                    return pltpu.roll(e, 1, 1)
                if g == 2:
                    return pltpu.roll(e, rows - 1, 1)
                return jnp.where(south, pltpu.roll(e, 1, 1), pltpu.roll(e, rows - 1, 1))

            now = [upwind_order(lambda side, q: column(q), p) for p in range(8)]
            rates = [upwind_order(spread(0), p) for p in range(1, 8)]
            seas = [upwind_order(spread(1), p) for p in range(1, 8)]
            keep = [None] + [sea - rate * (cos + sin) for sea, rate in zip(seas, rates)]
            from_x = [None] + [rate * cos for rate in rates]
            from_y = [None] + [rate * inner_sin for rate in rates]
            for t in range(1, PSTEPS + 1):
                now = [None] * t + [
                    keep[p] * now[p] + from_x[p] * now[p - 1] + from_y[p] * behind(now[p]) for p in range(t, 8)
                ]
            for p in range(PSTEPS, 8):
                result[p - PSTEPS, f * K + g * 8 : f * K + g * 8 + 8, :] = now[p]

    z = pos[0]
    width = rows // pos_count(parts)
    for out, (s, lo, size) in zip(outs, parts):
        at = pl.multiple_of(jnp.bitwise_xor(z, s) * width + lo, LANES)
        out[...] = result[:, :, pl.ds(at, size)].astype(jnp.bfloat16)


def pos_count(parts):
    return max(s for s, _, _ in parts) + 1


def propagate(z, spectrum, code, table, trig, parts, skip, steps, halo=None):
    columns, rows = spectrum.shape[1:]
    comps = steps * PAIR
    whole = lambda a: pl.BlockSpec(a.shape, lambda i, z: (0,) * a.ndim)
    blocked = lambda a, n: pl.BlockSpec((n,) + a.shape[1:], lambda i, z: (skip + i, 0, 0))
    args, specs = [spectrum], [blocked(spectrum, PAIR)]
    if halo is not None:
        west, east = halo
        last = pl.BlockSpec((1, columns, rows), lambda i, z: (west.shape[0] - 1, 0, 0))
        args += [west, east, code, west, east]
        specs += [blocked(west, K // 2), blocked(east, K // 2), whole(code), last, last]
    else:
        args += [code]
        specs += [whole(code)]
    args += [table, trig]
    specs += [whole(table), whole(trig)]
    return pl.pallas_call(
        functools.partial(propagate_kernel, halo is not None, parts, skip),
        grid_spec=pltpu.PrefetchScalarGridSpec(
            num_scalar_prefetch=1,
            grid=(steps,),
            in_specs=specs,
            out_specs=[pl.BlockSpec((4, PAIR, size), lambda i, z: (0, i, 0)) for _, _, size in parts],
            scratch_shapes=[
                pltpu.VMEM((rows // LANES, PAIR * columns, LANES), jnp.float32),
                pltpu.VMEM((4, columns, rows), jnp.float32),
                pltpu.VMEM((4, PAIR, rows), jnp.float32),
            ],
        ),
        out_shape=[jax.ShapeDtypeStruct((4, comps, size), jnp.bfloat16) for _, _, size in parts],
        compiler_params=pltpu.CompilerParams(vmem_limit_bytes=VMEM_LIMIT),
        cost_estimate=pl.CostEstimate(flops=comps * columns * rows * 30, bytes_accessed=6 * comps * rows * 8, transcendentals=0),
        name="propagate_downwind" if halo is None else "propagate_upwind",
    )(z, *args)


def rank_kernel(sea, ranks, most, mask):
    blocks, span = mask.shape
    width = span // 4
    for r in range(blocks):
        d, g = r // 2, r % 2
        for i in range(4):
            x = 4 + i if g else 3 - i
            mask[r : r + 1, i * width : (i + 1) * width] = sea[x : x + 1, d * width : (d + 1) * width].astype(jnp.float32)
    lane = lax.broadcasted_iota(jnp.int32, mask.shape, 1)
    count = mask[...]
    shift = 1
    while shift < span:
        count += jnp.where(lane >= shift, pltpu.roll(count, shift, 1), 0.0)
        shift *= 2
    place = jnp.where(mask[...] > 0.0, count - 1.0, -1.0).astype(jnp.int32)
    for r in range(blocks):
        ranks[r // 2, r % 2] = place[r : r + 1]
    top = jnp.max(jnp.max(count, axis=1, keepdims=True), axis=0, keepdims=True)
    most[...] = jnp.broadcast_to(top, most.shape).astype(jnp.int32)


def sea_ranks(sea_mask, count):
    span = 4 * (sea_mask.shape[1] // count)
    return pl.pallas_call(
        rank_kernel,
        out_shape=[
            jax.ShapeDtypeStruct((count, 2, 1, span), jnp.int32),
            jax.ShapeDtypeStruct((8, LANES), jnp.int32),
        ],
        scratch_shapes=[pltpu.VMEM((2 * count, span), jnp.float32)],
        cost_estimate=SHORT,
        name="sea_ranks",
    )(sea_mask)


def one_hot(rank, first, size):
    row = first + lax.broadcasted_iota(jnp.int32, (size, rank.shape[1]), 0)
    return jnp.where(row == rank, 1.0, 0.0).astype(jnp.bfloat16)


def pack(values, hot):
    return lax.dot_general(values, hot, (((1,), (1,)), ((), ())), preferred_element_type=jnp.float32)


def pack_points_kernel(downwind, first_block, pos, piece, ranks, *outs):
    comps = piece.shape[1]
    blocks = sum(out.shape[0] for out in outs)
    values = jnp.concatenate([piece[i if downwind else 3 - i] for i in range(4)], axis=1)
    low, high = (
        pack(values, one_hot(ranks[0, g], first_block * LANES, blocks * LANES)) for g in range(2)
    )
    if downwind:
        low, high = high, low
    packed = jnp.where(eastward_rows(0, comps), low, high).astype(jnp.bfloat16)
    at = 0
    for out in outs:
        for j in range(out.shape[0]):
            out[j] = packed[:, at * LANES : (at + 1) * LANES]
            at += 1


def pack_points(z, s, piece, ranks, downwind, first_block, sizes):
    comps = piece.shape[1]
    whole = lambda a: pl.BlockSpec(a.shape, lambda i, z: (0,) * a.ndim)
    outs = [jax.ShapeDtypeStruct((n, comps, LANES), jnp.bfloat16) for n in sizes]
    return pl.pallas_call(
        functools.partial(pack_points_kernel, downwind, first_block),
        grid_spec=pltpu.PrefetchScalarGridSpec(
            num_scalar_prefetch=1,
            grid=(1,),
            in_specs=[
                whole(piece),
                pl.BlockSpec((1,) + ranks.shape[1:], lambda i, z: (jnp.bitwise_xor(z[0], s), 0, 0, 0)),
            ],
            out_specs=[whole(out) for out in outs],
        ),
        out_shape=outs,
        compiler_params=pltpu.CompilerParams(vmem_limit_bytes=VMEM_LIMIT),
        cost_estimate=SHORT,
        name="pack_points",
    )(z, piece, ranks)


def pack_first_kernel(first_block, count, pos, *refs):
    pieces, (ranks, wind_c, wind_s, packed, wind) = refs[:-5], refs[-5:]
    z = pos[0]
    blocks, total, _ = packed.shape
    comps = total // count
    hots = [one_hot(ranks[0, g], first_block * LANES, blocks * LANES) for g in range(2)]
    mask = eastward_rows(0, comps)
    for s in range(count):
        at = pl.multiple_of(jnp.bitwise_xor(z, s) * comps, comps)
        values = jnp.concatenate([pieces[s][i] for i in range(4)], axis=1)
        low, high = (pack(values, hot) for hot in hots)
        both = jnp.where(mask, high, low).astype(jnp.bfloat16)
        for j in range(blocks):
            packed[j, pl.ds(at, comps), :] = both[:, j * LANES : (j + 1) * LANES]
    for g in range(2):
        parts = []
        for source in (wind_c, wind_s):
            left = jnp.concatenate([source[4 + i if g else 3 - i] for i in range(4)], axis=1)
            for _ in range(3):
                part = left.astype(jnp.bfloat16).astype(jnp.float32)
                parts.append(part)
                left = left - part
        parts += [jnp.zeros_like(left)] * 2
        row = pack(jnp.concatenate(parts, axis=0).astype(jnp.bfloat16), hots[g])
        for n in range(2):
            wind[2 * g + n] = row[3 * n : 3 * n + 1] + row[3 * n + 1 : 3 * n + 2] + row[3 * n + 2 : 3 * n + 3]


def pack_first(z, pieces, ranks, wind_c, wind_s, count, first_block, blocks):
    total = sum(piece.shape[1] for piece in pieces)
    whole = lambda a: pl.BlockSpec(a.shape, lambda i, z: (0,) * a.ndim)
    outs = [
        jax.ShapeDtypeStruct((blocks, total, LANES), jnp.bfloat16),
        jax.ShapeDtypeStruct((4, 1, blocks * LANES), jnp.float32),
    ]
    return pl.pallas_call(
        functools.partial(pack_first_kernel, first_block, count),
        grid_spec=pltpu.PrefetchScalarGridSpec(
            num_scalar_prefetch=1,
            grid=(1,),
            in_specs=[whole(piece) for piece in pieces]
            + [pl.BlockSpec((1,) + ranks.shape[1:], lambda i, z: (z[0], 0, 0, 0)), whole(wind_c), whole(wind_s)],
            out_specs=[whole(out) for out in outs],
        ),
        out_shape=outs,
        compiler_params=pltpu.CompilerParams(vmem_limit_bytes=VMEM_LIMIT),
        cost_estimate=pl.CostEstimate(flops=int(5.0e6 * 1153), bytes_accessed=1, transcendentals=0),
        name="pack_first",
    )(z, *pieces, ranks, wind_c, wind_s)


def sources_kernel(count, pos, *refs):
    first, later, refs = refs[0], refs[1 : 1 + count], refs[1 + count :]
    second, (winds, coupling, trig) = refs[:count], refs[count : count + 3]
    outs, (state, rounded, nonlin, wind) = refs[count + 3 : 2 * count + 3], refs[2 * count + 3 :]
    comps, width = second[0].shape[1:]
    z = pos[0]
    mask = eastward_rows(0, comps)
    for s in range(count):
        source = jnp.bitwise_xor(z, s)
        at = pl.ds(pl.multiple_of(source * comps, comps), comps)
        part = comps - later[s].shape[1]
        early = first[0, pl.ds(pl.multiple_of(source * part, part), part), :]
        down = jnp.concatenate([early, later[s][0]], axis=0).astype(jnp.float32)
        up = second[s][0].astype(jnp.float32)
        state[at, 0:width] = jnp.where(mask, up, down)
        state[at, width : 2 * width] = jnp.where(mask, down, up)
    for g in range(2):
        toward = trig[0, :, 0:1] * winds[2 * g] + trig[1, :, 0:1] * winds[2 * g + 1]
        wind[:, g * width : (g + 1) * width] = jnp.maximum(toward, 0.0)

    for step in range(SRC_STEPS):
        total = jnp.zeros((8, 2 * width), jnp.float32)
        for f in range(F):
            here = state[f * K : (f + 1) * K, :]
            rounded[f * K : (f + 1) * K, :] = here.astype(jnp.bfloat16)
            total += float(0.1 * 1.1**f) * (here[0:8] + here[8:16] + here[16:24])
        total = jnp.sum(total, axis=0, keepdims=True)
        sat = total / (total + 100.0)
        nonlin[...] = jnp.dot(coupling[...], rounded[...], preferred_element_type=jnp.float32)
        for f in range(F):
            at = slice(f * K, (f + 1) * K)
            here = state[at, :]
            damp = 1.0 - sat * float(0.15 * (f + 1) / F)
            gain = damp + wind[...] * float(1.1 ** (f - 16))
            state[at, :] = jnp.maximum(gain * here + 0.125 * nonlin[at, :], 0.0)

    for s in range(count):
        at = pl.ds(pl.multiple_of(jnp.bitwise_xor(z, s) * comps, comps), comps)
        for g in range(2):
            outs[s][g, 0] = state[at, g * width : (g + 1) * width].astype(jnp.bfloat16)


def sources(z, first, later, second, winds, coupling, trig, first_block, blocks):
    count = len(second)
    _, comps, width = second[0].shape
    total = comps * count
    whole = lambda a: pl.BlockSpec(a.shape, lambda i, z: (0,) * a.ndim)
    return pl.pallas_call(
        functools.partial(sources_kernel, count),
        grid_spec=pltpu.PrefetchScalarGridSpec(
            num_scalar_prefetch=1,
            grid=(blocks,),
            in_specs=[pl.BlockSpec((1,) + a.shape[1:], lambda i, z: (first_block + i, 0, 0)) for a in [first, *later]]
            + [
                pl.BlockSpec((1, comps, width), lambda i, z, at=0 if a.shape[0] == blocks else first_block: (at + i, 0, 0))
                for a in second
            ]
            + [pl.BlockSpec((4, 1, width), lambda i, z: (0, 0, first_block + i)), whole(coupling), whole(trig)],
            out_specs=[pl.BlockSpec((2, 1, comps, width), lambda i, z: (0, i, 0, 0))] * count,
            scratch_shapes=[
                pltpu.VMEM((total, 2 * width), jnp.float32),
                pltpu.VMEM((total, 2 * width), jnp.bfloat16),
                pltpu.VMEM((total, 2 * width), jnp.float32),
                pltpu.VMEM((K, 2 * width), jnp.float32),
            ],
        ),
        out_shape=[jax.ShapeDtypeStruct((2, blocks, comps, width), jnp.bfloat16)] * count,
        compiler_params=pltpu.CompilerParams(vmem_limit_bytes=VMEM_LIMIT),
        cost_estimate=pl.CostEstimate(
            flops=int(SRC_STEPS * 2 * total**2 * 2 * blocks * width / 1.0), bytes_accessed=1, transcendentals=0
        ),
        name="source_terms",
    )(z, first, *later, *second, winds, coupling, trig)


def unpack_kernel(partners, first_block, rest_block, scalars, *refs):
    n = len(partners)
    blocks, refs = refs[:n], refs[n:]
    rest = refs[:n] if rest_block else ()
    ranks, (out, turned) = refs[len(rest)], refs[-2:]
    comps, _, width = out.shape
    tiles = width // LANES

    def spread(part, first, add):
        for g in range(2):
            values = jnp.concatenate([part[g, j] for j in range(part.shape[1])], axis=1)
            hot = one_hot(ranks[0, g], first * LANES, values.shape[1])
            wide = jnp.dot(values, hot, preferred_element_type=jnp.float32)
            for i in range(4):
                x = 4 + i if g else 3 - i
                for t in range(tiles):
                    at = i * width + t * LANES
                    here = wide[:, at : at + LANES]
                    if add:
                        here += turned[t, pl.ds(x, comps, stride=8), :]
                    turned[t, pl.ds(x, comps, stride=8), :] = here

    for i in range(n):

        @pl.when(pl.program_id(0) == i)
        def _():
            spread(blocks[i], first_block, False)
            if rest:

                @pl.when(scalars[1] > 0)
                def _():
                    spread(rest[i], rest_block, True)

    for t in range(tiles):
        here = turned[t].reshape(comps, 8, LANES)
        if len(refs) > len(rest) + 3:
            here += refs[len(rest) + 1][:, :, t * LANES : (t + 1) * LANES].astype(jnp.float32)
        out[:, :, t * LANES : (t + 1) * LANES] = here.astype(jnp.bfloat16)


def unpack(scalars, partners, blocks, first_block, rest, rest_block, ranks, rows, into):
    comps = blocks[0].shape[2]
    width = ranks.shape[3] // 4
    whole = lambda a: pl.BlockSpec(a.shape, lambda i, z: (0,) * a.ndim)
    first = partners[0]
    device = lambda i, z: jnp.bitwise_xor(z[0], first + i)
    place = pl.BlockSpec((comps, 8, width), lambda i, z: (0, 0, device(i, z)))
    extra = [] if into is None else [into]
    inputs = [*blocks, *rest]
    return pl.pallas_call(
        functools.partial(unpack_kernel, partners, first_block, rest_block),
        grid_spec=pltpu.PrefetchScalarGridSpec(
            num_scalar_prefetch=1,
            grid=(len(partners),),
            in_specs=[whole(part) for part in inputs]
            + [pl.BlockSpec((1,) + ranks.shape[1:], lambda i, z: (device(i, z), 0, 0, 0))]
            + [place] * len(extra),
            out_specs=place,
            scratch_shapes=[pltpu.VMEM((width // LANES, comps * 8, LANES), jnp.float32)],
        ),
        out_shape=jax.ShapeDtypeStruct((comps, 8, rows), jnp.bfloat16),
        input_output_aliases={len(inputs) + 2: 0} if extra else {},
        compiler_params=pltpu.CompilerParams(vmem_limit_bytes=VMEM_LIMIT),
        cost_estimate=SHORT,
        name="unpack",
    )(scalars, *inputs, ranks, *extra)


def send(block, s, count):
    return lax.ppermute(block, "comp", [(i, i ^ s) for i in range(count)])


def exchange(blocks, axis):
    count = len(blocks)
    came = {s: send(blocks[s], s, count) for s in range(count - 1, 0, -1)}
    return [blocks[0]] + [came[s] for s in range(1, count)]


def exchange_rare(blocks, axis):
    order = jnp.bitwise_xor(lax.axis_index(axis), jnp.arange(len(blocks)))
    came = lax.all_to_all(jnp.stack(blocks)[order], axis, split_axis=0, concat_axis=0, tiled=True)[order]
    return [came[s] for s in range(len(blocks))]


def on_device(spectrum, sea_mask, depth_class, group_speed, wind_speed, wind_dir, coupling):
    comps, columns, rows = spectrum.shape
    count = lax.axis_size("comp")
    tiles = lax.axis_size("tile")
    place = lax.axis_index("comp")
    z = place.astype(jnp.int32).reshape(1)
    width = rows // count
    east = [(i, (i + 1) % tiles) for i in range(tiles)]
    west = [(j, i) for i, j in east]

    freqs = comps // K
    table = lax.dynamic_slice_in_dim(group_speed, place * freqs, freqs, 1).T
    table = jnp.pad(table, ((0, 0), (0, LANES - table.shape[1])))[:, None]
    trig = jnp.broadcast_to(jnp.asarray(np.stack([np.abs(COS), np.abs(SIN)]))[:, :, None], (2, K, LANES))
    signed = jnp.broadcast_to(jnp.asarray(np.stack([COS, SIN]))[:, :, None], (2, K, LANES))
    start = place * width

    to_east, to_west, code = pack_halo(spectrum, sea_mask, depth_class)
    halo = lax.ppermute(to_east, "tile", east), lax.ppermute(to_west, "tile", west)
    pairs = comps // PAIR
    half = pairs // 2
    blocks = 4 * width // LANES
    main = blocks * 3 // 4
    chunks = 2 if main % 2 == 0 else 1
    size = main // chunks
    parts = [(s, 0, width) for s in range(count)]
    first = propagate(z, spectrum, code, table, trig, parts, 0, half)
    first = list(first)
    sea_late, _ = lax.optimization_barrier((sea_mask, first[0]))
    ranks, most = sea_ranks(sea_late, count)
    first[1], _ = lax.optimization_barrier((first[1], ranks))
    first = exchange(first, "comp")
    later = propagate(z, spectrum, code, table, trig, parts, half, pairs - half)
    pack_later = lambda s, piece: pack_points(z, s, piece, ranks, True, 0, [main])[0]
    later = list(later)
    packed_later = {s: send(pack_later(s, later[s]), s, count) for s in range(count - 1, 1, -1)}
    second = propagate(z, spectrum, code, table, trig, parts, 0, pairs, halo)
    later[1], _ = lax.optimization_barrier((later[1], second[0]))
    packed_later[1] = send(pack_later(1, later[1]), 1, count)
    packed = [pack_points(z, s, second[s], ranks, False, 0, [main] if s == 1 else [size] * chunks) for s in range(count)]
    near = send(packed[1][0], 1, count)
    own, speed, direction, _ = lax.optimization_barrier((later[0], wind_speed, wind_dir, packed[1][0]))
    speed_part = 0.002 * lax.dynamic_slice_in_dim(speed, start, width, 1)
    dir_part = lax.dynamic_slice_in_dim(direction, start, width, 1)
    wind_c, wind_s = (speed_part * jnp.cos(dir_part))[:, None], (speed_part * jnp.sin(dir_part))[:, None]
    packed_later = [pack_later(0, own)] + [packed_later[s] for s in range(1, count)]
    packed_first, winds = pack_first(z, first, ranks, wind_c, wind_s, count, 0, main)

    def remainder(first, later, second, ranks, wind_c, wind_s, coupling):
        rest = blocks - main
        down, winds = pack_first(z, first, ranks, wind_c, wind_s, count, main, rest)
        low = [pack_points(z, s, later[s], ranks, True, main, [rest])[0] for s in range(count)]
        high = [pack_points(z, s, second[s], ranks, False, main, [rest])[0] for s in range(count)]
        low, high = exchange_rare(low, "comp"), exchange_rare(high, "comp")
        return exchange_rare(sources(z, down, low, high, winds, coupling, signed, 0, rest), "comp")

    def nothing(*args):
        return [jnp.zeros((2, blocks - main, comps, LANES), jnp.bfloat16)] * count

    updated = []
    for c in range(chunks):
        far = {s: send(packed[s][c], s, count) for s in range(count - 1, 1, -1)}
        arrived = [packed[0][c], near] + [far[s] for s in range(2, count)]
        sent = sources(z, packed_first, packed_later, arrived, winds, coupling, signed, c * size, size)
        updated.append(exchange(sent, "comp"))
        if c == 0:
            most, _ = lax.optimization_barrier((most, arrived[0]))
            full = lax.pmax(most[0, 0], "tile") > main * LANES
    full, _ = lax.optimization_barrier((full, sent[0]))
    rest = lax.cond(full, remainder, nothing, first, later, second, ranks, wind_c, wind_s, coupling)
    scalars = jnp.concatenate([z, full.astype(jnp.int32).reshape(1)])
    everyone = list(range(count))
    out = unpack(scalars, everyone, updated[0], 0, rest, main, ranks, rows, None)
    for partners in (everyone[: count // 2], everyone[count // 2 :]):
        for c in range(1, chunks):
            out = unpack(scalars, partners, [updated[c][s] for s in partners], c * size, [], 0, ranks, rows, out)
    return out


def solution(mesh):
    placed = (
        P("comp", "tile", None),
        P("tile", None),
        P("tile", None),
        P(),
        P("tile", None),
        P("tile", None),
        P(),
    )
    return jax.shard_map(
        on_device, mesh=mesh, in_specs=placed, out_specs=P("comp", "tile", None), check_vma=False
    )
```

```python
import functools
import math

import jax
import jax.numpy as jnp
import numpy as np
from jax import lax
from jax.experimental import pallas as pl
from jax.experimental.pallas import tpu as pltpu
from jax.sharding import PartitionSpec as P

K = 24
F = 32
PSTEPS = 4
SRC_STEPS = 4
PAIR = 2 * K
LANES = 128
VMEM_LIMIT = 48 * 1024 * 1024
SHORT = pl.CostEstimate(flops=1, bytes_accessed=1, transcendentals=0)

THETA = np.arange(K).astype(np.float32) * np.float32(2.0 * math.pi / K)
COS = np.cos(THETA)
SIN = np.sin(THETA)


def eastward_rows(start, count):
    k = lax.rem(start + lax.broadcasted_iota(jnp.int32, (count, 1), 0), K)
    return (k < 6) | (k >= 18)


def pack_kernel(raw, sea, depth, to_east, to_west, code):
    step = pl.program_id(0)
    code[...] = depth[...] + 16 * sea[...]
    for out, runs, low in ((to_east, ((0, 6), (18, 24)), 4), (to_west, ((6, 18),), 0)):
        at = step * (K // 2)
        for first, last in runs:
            one = raw[first:last].astype(jnp.float32)
            two = raw[K + first : K + last].astype(jnp.float32)
            row = lax.broadcasted_iota(jnp.int32, one.shape, 1)
            if low:
                both = jnp.where(row < 4, pltpu.roll(one, 4, 1), two)
            else:
                both = jnp.where(row < 4, one, pltpu.roll(two, 4, 1))
            out[pl.ds(at, last - first)] = both.astype(jnp.bfloat16)
            at += last - first
        out[out.shape[0] - 1] = code[...].astype(jnp.float32).astype(jnp.bfloat16)


def pack_halo(spectrum, sea_mask, depth_class):
    comps, columns, rows = spectrum.shape
    half = jax.ShapeDtypeStruct((comps // 4 + 1, columns, rows), jnp.bfloat16)
    block = pl.BlockSpec(half.shape, lambda i: (0, 0, 0))
    cells = pl.BlockSpec(sea_mask.shape, lambda i: (0, 0))
    return pl.pallas_call(
        pack_kernel,
        grid=(comps // PAIR,),
        in_specs=[
            pl.BlockSpec((PAIR, columns, rows), lambda i: (i, 0, 0)),
            cells,
            cells,
        ],
        out_specs=[block, block, cells],
        out_shape=[half, half, jax.ShapeDtypeStruct(sea_mask.shape, jnp.int32)],
        compiler_params=pltpu.CompilerParams(vmem_limit_bytes=60 * 1024 * 1024),
        name="pack_halo",
    )(spectrum, sea_mask, depth_class)


def propagate_kernel(with_halo, parts, skip, pos, *refs):
    if with_halo:
        raw, west, east, code, code_west, code_east, table, trig = refs[:8]
        refs = refs[8:]
    else:
        raw, code, table, trig = refs[:4]
        refs = refs[4:]
    outs, (cols, speed, result) = refs[: len(parts)], refs[len(parts) :]
    columns, rows = code.shape
    tiles = rows // LANES
    nfreq = table.shape[0]
    step = pl.program_id(0)
    row8 = lax.broadcasted_iota(jnp.int32, (columns, rows), 0)

    for f in range(2):
        for first, last, eastward in ((0, 6, True), (6, 18, False), (18, 24, True)):
            a, b = f * K + first, f * K + last
            own = raw[a:b].astype(jnp.float32)
            if with_halo:
                at = {0: 0, 6: 0, 18: 6}[first]
                side = (west if eastward else east)[at : at + last - first].astype(jnp.float32)
                row = lax.broadcasted_iota(jnp.int32, own.shape, 1)
                own = pltpu.roll(own, 4, 1)
                if eastward:
                    side = pltpu.roll(side, 4, 1) if f else side
                    own = jnp.where(row < 4, side, own)
                else:
                    side = side if f else pltpu.roll(side, 4, 1)
                    own = jnp.where(row < 4, own, side)
            own = own.reshape(-1, rows)
            for t in range(tiles):
                cols[t, a * 8 : b * 8, :] = own[:, t * LANES : (t + 1) * LANES]

    if with_halo:
        turned = pltpu.roll(code[...], 4, 0)
        codes = (
            jnp.where(row8 < 4, pltpu.roll(code_west[0].astype(jnp.float32).astype(jnp.int32), 4, 0), turned),
            jnp.where(row8 < 4, turned, pltpu.roll(code_east[0].astype(jnp.float32).astype(jnp.int32), 4, 0)),
        )
    else:
        codes = (code[...],)
    lane = lax.broadcasted_iota(jnp.int32, (8, rows), 1)
    freq0 = (skip + step) * 2
    for f in range(2):
        line = jnp.broadcast_to(table[freq0 + f], (8, LANES))
        for n, c in enumerate(codes):
            sea = (c >= 16).astype(jnp.float32)
            depth = jnp.bitwise_and(c, 15)
            looked = [
                jnp.take_along_axis(line, depth[:, t * LANES : (t + 1) * LANES], axis=1)
                for t in range(tiles)
            ]
            speed[2 * n] = jnp.concatenate(looked, axis=1) * sea
            speed[2 * n + 1] = sea
        last_n = len(codes) - 1
        for g in range(3):
            base = (f * K + g * 8) * 8

            def column(p):
                return jnp.concatenate(
                    [cols[t, pl.ds(base + p, 8, stride=8), :] for t in range(tiles)], axis=1
                )

            east_rows = eastward_rows(g * 8, 8)

            def upwind_order(get, p):
                if g == 1:
                    return get(1, 7 - p)
                return jnp.where(east_rows, get(0, p), get(1, 7 - p))

            def spread(which):
                def get(side, p):
                    n = side if last_n else 0
                    return jnp.broadcast_to(speed[2 * n + which, p : p + 1, :], (8, rows))

                return get

            k = g * 8 + lax.broadcasted_iota(jnp.int32, (8, rows), 0)
            south = k < 12
            cos = jnp.concatenate([trig[0, g * 8 : g * 8 + 8, :]] * tiles, axis=1)
            sin = jnp.concatenate([trig[1, g * 8 : g * 8 + 8, :]] * tiles, axis=1)
            edge = (south & (lane == 0)) | (~south & (lane == rows - 1))
            inner_sin = jnp.where(edge, 0.0, sin)

            def behind(e):
                if g == 0:
                    return pltpu.roll(e, 1, 1)
                if g == 2:
                    return pltpu.roll(e, rows - 1, 1)
                return jnp.where(south, pltpu.roll(e, 1, 1), pltpu.roll(e, rows - 1, 1))

            now = [upwind_order(lambda side, q: column(q), p) for p in range(8)]
            rates = [upwind_order(spread(0), p) for p in range(1, 8)]
            seas = [upwind_order(spread(1), p) for p in range(1, 8)]
            keep = [None] + [sea - rate * (cos + sin) for sea, rate in zip(seas, rates)]
            from_x = [None] + [rate * cos for rate in rates]
            from_y = [None] + [rate * inner_sin for rate in rates]
            for t in range(1, PSTEPS + 1):
                now = [None] * t + [
                    keep[p] * now[p] + from_x[p] * now[p - 1] + from_y[p] * behind(now[p]) for p in range(t, 8)
                ]
            for p in range(PSTEPS, 8):
                result[p - PSTEPS, f * K + g * 8 : f * K + g * 8 + 8, :] = now[p]

    z = pos[0]
    width = rows // pos_count(parts)
    for out, (s, lo, size) in zip(outs, parts):
        at = pl.multiple_of(jnp.bitwise_xor(z, s) * width + lo, LANES)
        out[...] = result[:, :, pl.ds(at, size)].astype(jnp.bfloat16)


def pos_count(parts):
    return max(s for s, _, _ in parts) + 1


def propagate(z, spectrum, code, table, trig, parts, skip, steps, halo=None):
    columns, rows = spectrum.shape[1:]
    comps = steps * PAIR
    whole = lambda a: pl.BlockSpec(a.shape, lambda i, z: (0,) * a.ndim)
    blocked = lambda a, n: pl.BlockSpec((n,) + a.shape[1:], lambda i, z: (skip + i, 0, 0))
    args, specs = [spectrum], [blocked(spectrum, PAIR)]
    if halo is not None:
        west, east = halo
        last = pl.BlockSpec((1, columns, rows), lambda i, z: (west.shape[0] - 1, 0, 0))
        args += [west, east, code, west, east]
        specs += [blocked(west, K // 2), blocked(east, K // 2), whole(code), last, last]
    else:
        args += [code]
        specs += [whole(code)]
    args += [table, trig]
    specs += [whole(table), whole(trig)]
    return pl.pallas_call(
        functools.partial(propagate_kernel, halo is not None, parts, skip),
        grid_spec=pltpu.PrefetchScalarGridSpec(
            num_scalar_prefetch=1,
            grid=(steps,),
            in_specs=specs,
            out_specs=[pl.BlockSpec((4, PAIR, size), lambda i, z: (0, i, 0)) for _, _, size in parts],
            scratch_shapes=[
                pltpu.VMEM((rows // LANES, PAIR * columns, LANES), jnp.float32),
                pltpu.VMEM((4, columns, rows), jnp.float32),
                pltpu.VMEM((4, PAIR, rows), jnp.float32),
            ],
        ),
        out_shape=[jax.ShapeDtypeStruct((4, comps, size), jnp.bfloat16) for _, _, size in parts],
        compiler_params=pltpu.CompilerParams(vmem_limit_bytes=VMEM_LIMIT),
        cost_estimate=pl.CostEstimate(flops=comps * columns * rows * 30, bytes_accessed=6 * comps * rows * 8, transcendentals=0),
        name="propagate_downwind" if halo is None else "propagate_upwind",
    )(z, *args)


def rank_kernel(sea, ranks, most, mask):
    blocks, span = mask.shape
    width = span // 4
    for r in range(blocks):
        d, g = r // 2, r % 2
        for i in range(4):
            x = 4 + i if g else 3 - i
            mask[r : r + 1, i * width : (i + 1) * width] = sea[x : x + 1, d * width : (d + 1) * width].astype(jnp.float32)
    lane = lax.broadcasted_iota(jnp.int32, mask.shape, 1)
    count = mask[...]
    shift = 1
    while shift < span:
        count += jnp.where(lane >= shift, pltpu.roll(count, shift, 1), 0.0)
        shift *= 2
    place = jnp.where(mask[...] > 0.0, count - 1.0, -1.0).astype(jnp.int32)
    for r in range(blocks):
        ranks[r // 2, r % 2] = place[r : r + 1]
    top = jnp.max(jnp.max(count, axis=1, keepdims=True), axis=0, keepdims=True)
    most[...] = jnp.broadcast_to(top, most.shape).astype(jnp.int32)


def sea_ranks(sea_mask, count):
    span = 4 * (sea_mask.shape[1] // count)
    return pl.pallas_call(
        rank_kernel,
        out_shape=[
            jax.ShapeDtypeStruct((count, 2, 1, span), jnp.int32),
            jax.ShapeDtypeStruct((8, LANES), jnp.int32),
        ],
        scratch_shapes=[pltpu.VMEM((2 * count, span), jnp.float32)],
        cost_estimate=SHORT,
        name="sea_ranks",
    )(sea_mask)


def one_hot(rank, first, size):
    row = first + lax.broadcasted_iota(jnp.int32, (size, rank.shape[1]), 0)
    return jnp.where(row == rank, 1.0, 0.0).astype(jnp.bfloat16)


def pack(values, hot):
    return lax.dot_general(values, hot, (((1,), (1,)), ((), ())), preferred_element_type=jnp.float32)


def pack_points_kernel(downwind, first_block, pos, piece, ranks, *outs):
    comps = piece.shape[1]
    blocks = sum(out.shape[0] for out in outs)
    values = jnp.concatenate([piece[i if downwind else 3 - i] for i in range(4)], axis=1)
    low, high = (
        pack(values, one_hot(ranks[0, g], first_block * LANES, blocks * LANES)) for g in range(2)
    )
    if downwind:
        low, high = high, low
    packed = jnp.where(eastward_rows(0, comps), low, high).astype(jnp.bfloat16)
    at = 0
    for out in outs:
        for j in range(out.shape[0]):
            out[j] = packed[:, at * LANES : (at + 1) * LANES]
            at += 1


def pack_points(z, s, piece, ranks, downwind, first_block, sizes):
    comps = piece.shape[1]
    whole = lambda a: pl.BlockSpec(a.shape, lambda i, z: (0,) * a.ndim)
    outs = [jax.ShapeDtypeStruct((n, comps, LANES), jnp.bfloat16) for n in sizes]
    return pl.pallas_call(
        functools.partial(pack_points_kernel, downwind, first_block),
        grid_spec=pltpu.PrefetchScalarGridSpec(
            num_scalar_prefetch=1,
            grid=(1,),
            in_specs=[
                whole(piece),
                pl.BlockSpec((1,) + ranks.shape[1:], lambda i, z: (jnp.bitwise_xor(z[0], s), 0, 0, 0)),
            ],
            out_specs=[whole(out) for out in outs],
        ),
        out_shape=outs,
        compiler_params=pltpu.CompilerParams(vmem_limit_bytes=VMEM_LIMIT),
        cost_estimate=SHORT,
        name="pack_points",
    )(z, piece, ranks)


def pack_first_kernel(first_block, count, pos, *refs):
    pieces, (ranks, wind_speed, wind_dir, packed, wind) = refs[:-5], refs[-5:]
    z = pos[0]
    blocks, total, _ = packed.shape
    comps = total // count
    hots = [one_hot(ranks[0, g], first_block * LANES, blocks * LANES) for g in range(2)]
    mask = eastward_rows(0, comps)
    for s in range(count):
        at = pl.multiple_of(jnp.bitwise_xor(z, s) * comps, comps)
        values = jnp.concatenate([pieces[s][i] for i in range(4)], axis=1)
        low, high = (pack(values, hot) for hot in hots)
        both = jnp.where(mask, high, low).astype(jnp.bfloat16)
        for j in range(blocks):
            packed[j, pl.ds(at, comps), :] = both[:, j * LANES : (j + 1) * LANES]
    width = ranks.shape[3] // 4
    here = pl.ds(pl.multiple_of(z * width, LANES), width)
    speed, direction = 0.002 * wind_speed[:, here], wind_dir[:, here]
    winds = speed * jnp.cos(direction), speed * jnp.sin(direction)
    for g in range(2):
        parts = []
        for source in winds:
            left = jnp.concatenate([source[x : x + 1] for x in (range(4, 8) if g else range(3, -1, -1))], axis=1)
            for _ in range(3):
                part = left.astype(jnp.bfloat16).astype(jnp.float32)
                parts.append(part)
                left = left - part
        parts += [jnp.zeros_like(left)] * 2
        row = pack(jnp.concatenate(parts, axis=0).astype(jnp.bfloat16), hots[g])
        for n in range(2):
            wind[2 * g + n] = row[3 * n : 3 * n + 1] + row[3 * n + 1 : 3 * n + 2] + row[3 * n + 2 : 3 * n + 3]


def pack_first(z, pieces, ranks, wind_speed, wind_dir, count, first_block, blocks):
    total = sum(piece.shape[1] for piece in pieces)
    whole = lambda a: pl.BlockSpec(a.shape, lambda i, z: (0,) * a.ndim)
    outs = [
        jax.ShapeDtypeStruct((blocks, total, LANES), jnp.bfloat16),
        jax.ShapeDtypeStruct((4, 1, blocks * LANES), jnp.float32),
    ]
    return pl.pallas_call(
        functools.partial(pack_first_kernel, first_block, count),
        grid_spec=pltpu.PrefetchScalarGridSpec(
            num_scalar_prefetch=1,
            grid=(1,),
            in_specs=[whole(piece) for piece in pieces]
            + [pl.BlockSpec((1,) + ranks.shape[1:], lambda i, z: (z[0], 0, 0, 0)), whole(wind_speed), whole(wind_dir)],
            out_specs=[whole(out) for out in outs],
        ),
        out_shape=outs,
        compiler_params=pltpu.CompilerParams(vmem_limit_bytes=VMEM_LIMIT),
        cost_estimate=pl.CostEstimate(flops=int(5.0e6 * 1153), bytes_accessed=1, transcendentals=0),
        name="pack_first",
    )(z, *pieces, ranks, wind_speed, wind_dir)


def sources_kernel(count, pos, *refs):
    first, later, refs = refs[0], refs[1 : 1 + count], refs[1 + count :]
    second, (winds, coupling, trig) = refs[:count], refs[count : count + 3]
    outs, (state, rounded, nonlin, wind) = refs[count + 3 : 2 * count + 3], refs[2 * count + 3 :]
    comps, width = second[0].shape[1:]
    z = pos[0]
    mask = eastward_rows(0, comps)
    for s in range(count):
        source = jnp.bitwise_xor(z, s)
        at = pl.ds(pl.multiple_of(source * comps, comps), comps)
        part = comps - later[s].shape[1]
        early = first[0, pl.ds(pl.multiple_of(source * part, part), part), :]
        down = jnp.concatenate([early, later[s][0]], axis=0).astype(jnp.float32)
        up = second[s][0].astype(jnp.float32)
        state[at, 0:width] = jnp.where(mask, up, down)
        state[at, width : 2 * width] = jnp.where(mask, down, up)
    for g in range(2):
        toward = trig[0, :, 0:1] * winds[2 * g] + trig[1, :, 0:1] * winds[2 * g + 1]
        wind[:, g * width : (g + 1) * width] = jnp.maximum(toward, 0.0)

    for step in range(SRC_STEPS):
        total = jnp.zeros((8, 2 * width), jnp.float32)
        for f in range(F):
            here = state[f * K : (f + 1) * K, :]
            rounded[f * K : (f + 1) * K, :] = here.astype(jnp.bfloat16)
            total += float(0.1 * 1.1**f) * (here[0:8] + here[8:16] + here[16:24])
        total = jnp.sum(total, axis=0, keepdims=True)
        sat = total / (total + 100.0)
        nonlin[...] = jnp.dot(coupling[...], rounded[...], preferred_element_type=jnp.float32)
        for f in range(F):
            at = slice(f * K, (f + 1) * K)
            here = state[at, :]
            damp = 1.0 - sat * float(0.15 * (f + 1) / F)
            gain = damp + wind[...] * float(1.1 ** (f - 16))
            state[at, :] = jnp.maximum(gain * here + 0.125 * nonlin[at, :], 0.0)

    for s in range(count):
        at = pl.ds(pl.multiple_of(jnp.bitwise_xor(z, s) * comps, comps), comps)
        for g in range(2):
            outs[s][g, 0] = state[at, g * width : (g + 1) * width].astype(jnp.bfloat16)


def sources(z, first, later, second, winds, coupling, trig, first_block, blocks):
    count = len(second)
    _, comps, width = second[0].shape
    total = comps * count
    whole = lambda a: pl.BlockSpec(a.shape, lambda i, z: (0,) * a.ndim)
    return pl.pallas_call(
        functools.partial(sources_kernel, count),
        grid_spec=pltpu.PrefetchScalarGridSpec(
            num_scalar_prefetch=1,
            grid=(blocks,),
            in_specs=[pl.BlockSpec((1,) + a.shape[1:], lambda i, z: (first_block + i, 0, 0)) for a in [first, *later]]
            + [
                pl.BlockSpec((1, comps, width), lambda i, z, at=0 if a.shape[0] == blocks else first_block: (at + i, 0, 0))
                for a in second
            ]
            + [pl.BlockSpec((4, 1, width), lambda i, z: (0, 0, first_block + i)), whole(coupling), whole(trig)],
            out_specs=[pl.BlockSpec((2, 1, comps, width), lambda i, z: (0, i, 0, 0))] * count,
            scratch_shapes=[
                pltpu.VMEM((total, 2 * width), jnp.float32),
                pltpu.VMEM((total, 2 * width), jnp.bfloat16),
                pltpu.VMEM((total, 2 * width), jnp.float32),
                pltpu.VMEM((K, 2 * width), jnp.float32),
            ],
        ),
        out_shape=[jax.ShapeDtypeStruct((2, blocks, comps, width), jnp.bfloat16)] * count,
        compiler_params=pltpu.CompilerParams(vmem_limit_bytes=VMEM_LIMIT),
        cost_estimate=pl.CostEstimate(
            flops=int(SRC_STEPS * 2 * total**2 * 2 * blocks * width / 1.0), bytes_accessed=1, transcendentals=0
        ),
        name="source_terms",
    )(z, first, *later, *second, winds, coupling, trig)


def unpack_kernel(partners, first_block, rest_block, scalars, *refs):
    n = len(partners)
    blocks, refs = refs[:n], refs[n:]
    rest = refs[:n] if rest_block else ()
    ranks, (out, turned) = refs[len(rest)], refs[-2:]
    comps, _, width = out.shape
    tiles = width // LANES

    def spread(part, first, add):
        for g in range(2):
            values = jnp.concatenate([part[g, j] for j in range(part.shape[1])], axis=1)
            hot = one_hot(ranks[0, g], first * LANES, values.shape[1])
            wide = jnp.dot(values, hot, preferred_element_type=jnp.float32)
            for i in range(4):
                x = 4 + i if g else 3 - i
                for t in range(tiles):
                    at = i * width + t * LANES
                    here = wide[:, at : at + LANES]
                    if add:
                        here += turned[t, pl.ds(x, comps, stride=8), :]
                    turned[t, pl.ds(x, comps, stride=8), :] = here

    for i in range(n):

        @pl.when(pl.program_id(0) == i)
        def _():
            spread(blocks[i], first_block, False)
            if rest:

                @pl.when(scalars[1] > 0)
                def _():
                    spread(rest[i], rest_block, True)

    for t in range(tiles):
        here = turned[t].reshape(comps, 8, LANES)
        if len(refs) > len(rest) + 3:
            here += refs[len(rest) + 1][:, :, t * LANES : (t + 1) * LANES].astype(jnp.float32)
        out[:, :, t * LANES : (t + 1) * LANES] = here.astype(jnp.bfloat16)


def unpack(scalars, partners, blocks, first_block, rest, rest_block, ranks, rows, into):
    comps = blocks[0].shape[2]
    width = ranks.shape[3] // 4
    whole = lambda a: pl.BlockSpec(a.shape, lambda i, z: (0,) * a.ndim)
    first = partners[0]
    device = lambda i, z: jnp.bitwise_xor(z[0], first + i)
    place = pl.BlockSpec((comps, 8, width), lambda i, z: (0, 0, device(i, z)))
    extra = [] if into is None else [into]
    inputs = [*blocks, *rest]
    return pl.pallas_call(
        functools.partial(unpack_kernel, partners, first_block, rest_block),
        grid_spec=pltpu.PrefetchScalarGridSpec(
            num_scalar_prefetch=1,
            grid=(len(partners),),
            in_specs=[whole(part) for part in inputs]
            + [pl.BlockSpec((1,) + ranks.shape[1:], lambda i, z: (device(i, z), 0, 0, 0))]
            + [place] * len(extra),
            out_specs=place,
            scratch_shapes=[pltpu.VMEM((width // LANES, comps * 8, LANES), jnp.float32)],
        ),
        out_shape=jax.ShapeDtypeStruct((comps, 8, rows), jnp.bfloat16),
        input_output_aliases={len(inputs) + 2: 0} if extra else {},
        compiler_params=pltpu.CompilerParams(vmem_limit_bytes=VMEM_LIMIT),
        cost_estimate=SHORT,
        name="unpack",
    )(scalars, *inputs, ranks, *extra)


def send(block, s, count):
    return lax.ppermute(block, "comp", [(i, i ^ s) for i in range(count)])


def exchange(blocks, axis):
    count = len(blocks)
    came = {s: send(blocks[s], s, count) for s in range(count - 1, 0, -1)}
    return [blocks[0]] + [came[s] for s in range(1, count)]


def exchange_rare(blocks, axis):
    order = jnp.bitwise_xor(lax.axis_index(axis), jnp.arange(len(blocks)))
    came = lax.all_to_all(jnp.stack(blocks)[order], axis, split_axis=0, concat_axis=0, tiled=True)[order]
    return [came[s] for s in range(len(blocks))]


def on_device(spectrum, sea_mask, depth_class, group_speed, wind_speed, wind_dir, coupling):
    comps, columns, rows = spectrum.shape
    count = lax.axis_size("comp")
    tiles = lax.axis_size("tile")
    place = lax.axis_index("comp")
    z = place.astype(jnp.int32).reshape(1)
    width = rows // count
    east = [(i, (i + 1) % tiles) for i in range(tiles)]
    west = [(j, i) for i, j in east]

    freqs = comps // K
    table = lax.dynamic_slice_in_dim(group_speed, place * freqs, freqs, 1).T
    table = jnp.pad(table, ((0, 0), (0, LANES - table.shape[1])))[:, None]
    trig = jnp.broadcast_to(jnp.asarray(np.stack([np.abs(COS), np.abs(SIN)]))[:, :, None], (2, K, LANES))
    signed = jnp.broadcast_to(jnp.asarray(np.stack([COS, SIN]))[:, :, None], (2, K, LANES))

    to_east, to_west, code = pack_halo(spectrum, sea_mask, depth_class)
    halo = lax.ppermute(to_east, "tile", east), lax.ppermute(to_west, "tile", west)
    pairs = comps // PAIR
    half = pairs // 2
    blocks = 4 * width // LANES
    main = blocks * 3 // 4
    chunks = 2 if main % 2 == 0 else 1
    size = main // chunks
    parts = [(s, 0, width) for s in range(count)]
    first = propagate(z, spectrum, code, table, trig, parts, 0, half)
    first = list(first)
    sea_late, _ = lax.optimization_barrier((sea_mask, first[0]))
    ranks, most = sea_ranks(sea_late, count)
    first[1], _ = lax.optimization_barrier((first[1], ranks))
    first = exchange(first, "comp")
    later = propagate(z, spectrum, code, table, trig, parts, half, pairs - half)
    pack_later = lambda s, piece: pack_points(z, s, piece, ranks, True, 0, [main])[0]
    later = list(later)
    packed_later = {s: send(pack_later(s, later[s]), s, count) for s in range(count - 1, 1, -1)}
    second = propagate(z, spectrum, code, table, trig, parts, 0, pairs, halo)
    later[1], _ = lax.optimization_barrier((later[1], second[0]))
    packed_later[1] = send(pack_later(1, later[1]), 1, count)
    packed = [pack_points(z, s, second[s], ranks, False, 0, [main] if s == 1 else [size] * chunks) for s in range(count)]
    near = send(packed[1][0], 1, count)
    own, _ = lax.optimization_barrier((later[0], packed[1][0]))
    packed_later = [pack_later(0, own)] + [packed_later[s] for s in range(1, count)]
    packed_first, winds = pack_first(z, first, ranks, wind_speed, wind_dir, count, 0, main)

    def remainder(first, later, second, ranks, wind_speed, wind_dir, coupling):
        rest = blocks - main
        down, winds = pack_first(z, first, ranks, wind_speed, wind_dir, count, main, rest)
        low = [pack_points(z, s, later[s], ranks, True, main, [rest])[0] for s in range(count)]
        high = [pack_points(z, s, second[s], ranks, False, main, [rest])[0] for s in range(count)]
        low, high = exchange_rare(low, "comp"), exchange_rare(high, "comp")
        return exchange_rare(sources(z, down, low, high, winds, coupling, signed, 0, rest), "comp")

    def nothing(*args):
        return [jnp.zeros((2, blocks - main, comps, LANES), jnp.bfloat16)] * count

    updated = []
    for c in range(chunks):
        far = {s: send(packed[s][c], s, count) for s in range(count - 1, 1, -1)}
        arrived = [packed[0][c], near] + [far[s] for s in range(2, count)]
        sent = sources(z, packed_first, packed_later, arrived, winds, coupling, signed, c * size, size)
        updated.append(exchange(sent, "comp"))
        if c == 0:
            most, _ = lax.optimization_barrier((most, arrived[0]))
            full = lax.pmax(most[0, 0], "tile") > main * LANES
    full, _ = lax.optimization_barrier((full, sent[0]))
    rest = lax.cond(full, remainder, nothing, first, later, second, ranks, wind_speed, wind_dir, coupling)
    scalars = jnp.concatenate([z, full.astype(jnp.int32).reshape(1)])
    everyone = list(range(count))
    out = unpack(scalars, everyone, updated[0], 0, rest, main, ranks, rows, None)
    for partners in (everyone[: count // 2], everyone[count // 2 :]):
        for c in range(1, chunks):
            out = unpack(scalars, partners, [updated[c][s] for s in partners], c * size, [], 0, ranks, rows, out)
    return out


def solution(mesh):
    placed = (
        P("comp", "tile", None),
        P("tile", None),
        P("tile", None),
        P(),
        P("tile", None),
        P("tile", None),
        P(),
    )
    return jax.shard_map(
        on_device, mesh=mesh, in_specs=placed, out_specs=P("comp", "tile", None), check_vma=False
    )
```
